1024 devices in a mesh: expert: 16 (over y, core), tensor: 16 (over z), dp: 4 (over x).
Axes of the slice: x: 4, y: 8, z: 16, core: 2. Of those that a mesh axis runs over, the one named last changes fastest.
Arguments:
- cotangent: bfloat16 [64, 128, 7168], P(('expert', 'dp'), 'tensor'), may hold values from -6 to 6
- routed_expert_index: int32 [64, 128, 8], P(('expert', 'dp')), may hold values from 0 to 127, all different within a row; in each aligned block of 128 rows (0 to 127, 128 to 255, ..., all dimensions but the last counted through in order) at most 12 rows name the same one
- chosen_gate_weight: float32 [64, 128, 8], P(('expert', 'dp')), may hold values from 0.05 to 0.6
- routed_down_weight: bfloat16 [128, 1024, 7168], P(('expert', 'dp'), None, 'tensor'), may hold values from -0.1875 to 0.1875
- routed_adapter_input_map: bfloat16 [128, 1024, 16], P(('expert', 'dp'), 'tensor'), may hold values from -0.1875 to 0.1875
- routed_adapter_output_map: bfloat16 [128, 16, 7168], P(('expert', 'dp'), None, 'tensor'), may hold values from -0.0625 to 0.0625
- routed_gate_saved: bfloat16 [1024, 128, 768], P('tensor', ('expert', 'dp')), may hold values from -6 to 6
- routed_up_saved: bfloat16 [1024, 128, 768], P('tensor', ('expert', 'dp')), may hold values from -6 to 6
- shared_down_weight: bfloat16 [2048, 7168], P('tensor'), may hold values from -0.125 to 0.125
- shared_adapter_input_map: bfloat16 [2048, 16], P('tensor'), may hold values from -0.125 to 0.125
- shared_adapter_output_map: bfloat16 [16, 7168], replicated, may hold values from -0.0625 to 0.0625
- shared_gate_saved: bfloat16 [64, 128, 2048], P(('expert', 'dp'), None, 'tensor'), may hold values from -6 to 6
- shared_up_saved: bfloat16 [64, 128, 2048], P(('expert', 'dp'), None, 'tensor'), may hold values from -6 to 6
Outputs:
- grad_gate_routed: bfloat16 [1024, 128, 768], P('tensor', ('expert', 'dp'))
- grad_up_routed: bfloat16 [1024, 128, 768], P('tensor', ('expert', 'dp'))
- grad_gate_shared: bfloat16 [64, 128, 2048], P(('expert', 'dp'), None, 'tensor')
- grad_up_shared: bfloat16 [64, 128, 2048], P(('expert', 'dp'), None, 'tensor')
- grad_a_routed: float32 [128, 1024, 16], P(('expert', 'dp'), 'tensor')
- grad_b_routed: float32 [128, 16, 7168], P(('expert', 'dp'), None, 'tensor')
- grad_a_shared: float32 [2048, 16], P('tensor')
- grad_b_shared: float32 [16, 7168], P(None, 'tensor')
The draws below stay inside these ranges and needn't reach their ends.
Inputs may be any that keep to these rules, and one draw needn't show every extreme that they name: `routed_expert_index`: each token names 8 different experts; within one token group no expert is named by more than 12 tokens, and in some group one expert is named by exactly 12.
All inputs are finite; a program needn't handle non-finite values.
Results may differ from the reference program's by a relative error of at most 0.024.
Values may be sent and summed in bfloat16 or wider, within the bound.
No kernel may reach another device: no remote copies, remote signals or barrier semaphores. Data moves between devices by JAX's collectives and lax.ppermute only.
A program may use at most 64 MiB of HBM per device.

```python
import math
import jax
import jax.numpy as jnp
import numpy as np
from jax import lax

MODEL_WIDTH = 7168
EXPERT_HIDDEN = 1024
SHARED_HIDDEN = 2048
ADAPTER_RANK = 16
TOPK = 8
TOK_GRP = 128
TOKEN_GROUPS = 64
ROUTED_EXPERTS = 128
CAP = 12
SLOTS = 768
FEAT_BLK = 448
N_TENSOR = 16


def block_scale(own_key, dims, cuts, low, high):
    level = 1.0
    for position, shards_of in cuts:
        draws = jax.random.uniform(jax.random.fold_in(jax.random.fold_in(own_key, 6), position), (shards_of,), jnp.float32, low / len(cuts), high / len(cuts))
        level = level * jnp.repeat(jnp.exp(draws), dims[position] // shards_of).reshape((-1,) + (1,) * (len(dims) - 1 - position))
    return level


def deal_out(rng, own, number, rows, amount, top, bound, skew):
    ranking = jax.random.permutation(rng, amount)
    heavy_load, usual = portions_of(amount, rows * top, bound, skew, True), portions_of(amount, rows * top, bound, skew, False)
    places = jnp.arange(amount)

    def named(sizes, turn):
        used = int((sizes > 0).sum())
        fixed = max(1, used // 4)
        moved = fixed + (places - fixed + turn * (used - fixed)) % max(1, amount - fixed)
        return jnp.zeros((amount,), jnp.int32).at[ranking[jnp.where(places < fixed, places, moved)]].set(jnp.asarray(sizes, jnp.int32))

    sizes = jnp.where(number % 4 == 0, named(heavy_load, number // 4), named(usual, number - number // 4 - 1))
    mixed = jax.random.permutation(jax.random.fold_in(own, 3), amount)
    donor, receiver = mixed[0:amount // 2 * 2:2], mixed[1:amount // 2 * 2:2]
    margin = jnp.minimum(sizes[donor] - 1, bound - sizes[receiver]) // 2
    margin = jnp.where((donor == ranking[0]) | (receiver == ranking[0]) | (sizes[receiver] == 0), 0, jnp.maximum(margin, 0))
    moved = jax.random.randint(jax.random.fold_in(own, 4), (amount // 2,), 0, 1 << 20) % (margin + 1)
    sizes = sizes.at[donor].add(-moved).at[receiver].add(moved)
    labels = jnp.searchsorted(jnp.cumsum(sizes), jnp.arange(rows * top), side="right").astype(jnp.int32)
    table = labels.reshape(top, rows).T
    table = table[jax.random.permutation(jax.random.fold_in(own, 1), rows)]
    turn = jax.random.randint(jax.random.fold_in(own, 2), (rows, 1), 0, top)
    return jnp.take_along_axis(table, (jnp.arange(top)[None, :] + turn) % top, axis=1)


def portions_of(amount, total, most, lean, full):
    weights = [(1 << 20) // math.isqrt(rank ** lean) + 1 for rank in range(1, amount + 1)]
    largest = most if full else min(most, max(-(-total // amount), total * weights[0] // sum(weights)))
    least = 1 if total - largest >= amount - 1 else 0
    given, surplus = [largest] + [least] * (amount - 1), total - largest - least * (amount - 1)
    while surplus > 0:
        candidates = [i for i in range(1, amount) if given[i] < largest] or [i for i in range(1, amount) if given[i] < most]
        pool, left = sum([weights[i] for i in candidates]), surplus
        for i in candidates:
            addition = min(most - given[i], max(1, left * weights[i] // pool), surplus)
            given[i] = given[i] + addition
            surplus = surplus - addition
    return np.array(given)


def gaussian(key, dims, deviation, limit, cuts=(), kind=jnp.bfloat16):
    drawn = jax.random.normal(key, dims, jnp.float32) * deviation
    if len(cuts) > 0:
        drawn = block_scale(key, dims, cuts, -0.22, 0.18) * drawn
    return jnp.clip(drawn, min=-limit, max=limit).astype(kind)


def setup_inputs(seed: int = 0) -> dict:
    key_of = jax.random.split(jax.random.key(seed), 14)
    cotangent = gaussian(key_of[0], (TOKEN_GROUPS, TOK_GRP, MODEL_WIDTH), 1.0, 6.0, ((0, 64), (1, 16)))
    routed_expert_index_keys = jax.random.split(jax.random.fold_in(key_of[1], 1), TOKEN_GROUPS * TOK_GRP // TOK_GRP)
    routed_expert_index_turns = jax.random.permutation(jax.random.fold_in(key_of[1], 3), TOKEN_GROUPS * TOK_GRP // TOK_GRP)
    routed_expert_index = jax.vmap(lambda own, number: deal_out(jax.random.fold_in(key_of[1], 2), own, number, TOK_GRP, ROUTED_EXPERTS, TOPK, CAP, 2))(routed_expert_index_keys, routed_expert_index_turns).reshape((TOKEN_GROUPS, TOK_GRP, TOPK))
    chosen_gate_weight = jnp.clip(0.05 + 0.55 * jax.random.uniform(key_of[2], (TOKEN_GROUPS, TOK_GRP, TOPK), jnp.float32) ** block_scale(key_of[2], (TOKEN_GROUPS, TOK_GRP, TOPK), ((0, 64),), -0.2, 0.2), 0.05, 0.6)
    routed_down_weight = gaussian(key_of[3], (ROUTED_EXPERTS, EXPERT_HIDDEN, MODEL_WIDTH), EXPERT_HIDDEN ** -0.5, 0.1875, ((0, 64), (2, 16)))
    routed_adapter_input_map = gaussian(key_of[4], (ROUTED_EXPERTS, EXPERT_HIDDEN, ADAPTER_RANK), EXPERT_HIDDEN ** -0.5, 0.1875, ((0, 64), (1, 16)))
    routed_adapter_output_map = gaussian(key_of[5], (ROUTED_EXPERTS, ADAPTER_RANK, MODEL_WIDTH), MODEL_WIDTH ** -0.5, 0.0625, ((0, 64), (2, 16)))
    routed_gate_saved = gaussian(key_of[6], (EXPERT_HIDDEN, ROUTED_EXPERTS, SLOTS), 1.0, 6.0, ((0, 16), (1, 64)))
    routed_up_saved = gaussian(key_of[7], (EXPERT_HIDDEN, ROUTED_EXPERTS, SLOTS), 1.0, 6.0, ((0, 16), (1, 64)))
    shared_down_weight = gaussian(key_of[8], (SHARED_HIDDEN, MODEL_WIDTH), SHARED_HIDDEN ** -0.5, 0.125, ((0, 16),))
    shared_adapter_input_map = gaussian(key_of[9], (SHARED_HIDDEN, ADAPTER_RANK), SHARED_HIDDEN ** -0.5, 0.125, ((0, 16),))
    shared_adapter_output_map = gaussian(key_of[10], (ADAPTER_RANK, MODEL_WIDTH), MODEL_WIDTH ** -0.5, 0.0625)
    shared_gate_saved = gaussian(key_of[11], (TOKEN_GROUPS, TOK_GRP, SHARED_HIDDEN), 1.0, 6.0, ((0, 64), (2, 16)))
    shared_up_saved = gaussian(key_of[12], (TOKEN_GROUPS, TOK_GRP, SHARED_HIDDEN), 1.0, 6.0, ((0, 64), (2, 16)))
    return dict(cotangent=cotangent, routed_expert_index=routed_expert_index, chosen_gate_weight=chosen_gate_weight, routed_down_weight=routed_down_weight, routed_adapter_input_map=routed_adapter_input_map, routed_adapter_output_map=routed_adapter_output_map, routed_gate_saved=routed_gate_saved, routed_up_saved=routed_up_saved, shared_down_weight=shared_down_weight, shared_adapter_input_map=shared_adapter_input_map, shared_adapter_output_map=shared_adapter_output_map, shared_gate_saved=shared_gate_saved, shared_up_saved=shared_up_saved)


ADAPTER_SCALE = 2.0


def swiglu_parts(gate_value, up_value):
    gate_float = gate_value.astype(jnp.float32)
    up_float = up_value.astype(jnp.float32)
    sigmoid_gate = jax.nn.sigmoid(gate_float)
    activated = gate_float * sigmoid_gate
    hidden_state = (activated * up_float).astype(jnp.bfloat16)
    gate_factor = up_float * sigmoid_gate * (1.0 + gate_float * (1.0 - sigmoid_gate))
    return hidden_state, gate_factor, activated


def group_lookup(group_ids, group_weights):
    flattened = group_ids.reshape(-1)
    onehot = (flattened[:, None] == jnp.arange(ROUTED_EXPERTS, dtype=jnp.int32)[None, :]).astype(jnp.int32)
    before = jnp.cumsum(onehot, axis=0) - onehot
    slot_index = jnp.sum(before * onehot, axis=1).astype(jnp.int32)
    token_index = jnp.repeat(jnp.arange(TOK_GRP, dtype=jnp.int32), TOPK)
    owner = jnp.full((ROUTED_EXPERTS, CAP), TOK_GRP, jnp.int32).at[flattened, slot_index].set(token_index)
    scale_factor = jnp.zeros((ROUTED_EXPERTS, CAP), jnp.float32).at[flattened, slot_index].set(group_weights.reshape(-1).astype(jnp.float32))
    return owner, scale_factor


def pick_rows(group_rows, owner_rows):
    return group_rows[owner_rows]


def reference(cotangent, routed_expert_index, chosen_gate_weight, routed_down_weight, routed_adapter_input_map, routed_adapter_output_map, routed_gate_saved, routed_up_saved, shared_down_weight, shared_adapter_input_map, shared_adapter_output_map, shared_gate_saved, shared_up_saved):
    owning_experts, scale_factors = jax.vmap(group_lookup)(routed_expert_index, chosen_gate_weight)
    padded = jnp.concatenate([cotangent, jnp.zeros((TOKEN_GROUPS, 1, MODEL_WIDTH), cotangent.dtype)], axis=1)
    weight_scale_factor = ADAPTER_SCALE / TOKEN_GROUPS

    def expert_backward(expert_slot):
        owner = owning_experts[:, expert_slot, :]
        scale_factor = scale_factors[:, expert_slot, :]
        picked = jax.vmap(pick_rows)(padded, owner)
        routed_output = (scale_factor[:, :, None] * picked.astype(jnp.float32)).astype(jnp.bfloat16).reshape(SLOTS, MODEL_WIDTH)
        routed_single_precision = routed_output.astype(jnp.float32)
        weight_float = routed_down_weight[expert_slot].astype(jnp.float32)
        parts = jnp.einsum("sjd,fjd->jfs", routed_single_precision.reshape(SLOTS, N_TENSOR, FEAT_BLK), weight_float.reshape(EXPERT_HIDDEN, N_TENSOR, FEAT_BLK))
        parts = lax.optimization_barrier(parts.astype(jnp.bfloat16)).astype(jnp.float32)
        hidden_gradient = jnp.sum(parts, axis=0)
        adapter_input = routed_adapter_input_map[expert_slot].astype(jnp.float32)
        rank_cast_back = jnp.einsum("bg,hg->hb", routed_single_precision, routed_adapter_output_map[expert_slot].astype(jnp.float32)).astype(jnp.bfloat16)
        rank_single_precision = rank_cast_back.astype(jnp.float32)
        hidden_gradient = hidden_gradient + ADAPTER_SCALE * jnp.einsum("cj,dc->dj", rank_single_precision, adapter_input)
        hidden_state, gate_factor, activated = swiglu_parts(routed_gate_saved[:, expert_slot, :], routed_up_saved[:, expert_slot, :])
        hidden_float = hidden_state.astype(jnp.float32)
        inner_cast_back = jnp.einsum("fs,fr->rs", hidden_float, adapter_input).astype(jnp.bfloat16)
        grad_a = weight_scale_factor * jnp.einsum("fs,rs->fr", hidden_float, rank_single_precision)
        grad_b = weight_scale_factor * jnp.einsum("rs,sd->rd", inner_cast_back.astype(jnp.float32), routed_single_precision)
        return (hidden_gradient * gate_factor).astype(jnp.bfloat16), (hidden_gradient * activated).astype(jnp.bfloat16), grad_a, grad_b

    gate_grads, up_grads, grad_a_routed, grad_b_routed = lax.map(expert_backward, jnp.arange(ROUTED_EXPERTS, dtype=jnp.int32))
    grad_gate_routed = jnp.transpose(gate_grads, (1, 0, 2))
    grad_up_routed = jnp.transpose(up_grads, (1, 0, 2))

    def shared_group(inputs):
        token_row_block, gate_value, up_value = inputs
        hidden_gradient = jnp.dot(token_row_block, shared_down_weight.T, preferred_element_type=jnp.float32)
        rank_cast_back = jnp.dot(token_row_block, shared_adapter_output_map.T, preferred_element_type=jnp.float32).astype(jnp.bfloat16)
        hidden_gradient = hidden_gradient + ADAPTER_SCALE * jnp.dot(rank_cast_back, shared_adapter_input_map.T, preferred_element_type=jnp.float32)
        hidden_state, gate_factor, activated = swiglu_parts(gate_value, up_value)
        inner_cast_back = jnp.dot(hidden_state, shared_adapter_input_map, preferred_element_type=jnp.float32).astype(jnp.bfloat16)
        term_a = jnp.dot(hidden_state.T, rank_cast_back, preferred_element_type=jnp.float32)
        term_b = jnp.dot(inner_cast_back.T, token_row_block, preferred_element_type=jnp.float32)
        return (hidden_gradient * gate_factor).astype(jnp.bfloat16), (hidden_gradient * activated).astype(jnp.bfloat16), term_a, term_b

    grad_gate_shared, grad_up_shared, terms_a, terms_b = lax.map(shared_group, (cotangent, shared_gate_saved, shared_up_saved))
    grad_a_shared = weight_scale_factor * jnp.sum(terms_a, axis=0)
    grad_b_shared = weight_scale_factor * jnp.sum(terms_b, axis=0)
    return (grad_gate_routed, grad_up_routed, grad_gate_shared, grad_up_shared, grad_a_routed, grad_b_routed, grad_a_shared, grad_b_shared)
```

```python
import jax
import jax.numpy as jnp
from jax import lax
from jax.experimental import pallas as pl
from jax.experimental.pallas import tpu as pltpu
from jax.sharding import PartitionSpec as P

ADAPTER_SCALE = 2.0
F32 = jnp.float32
BF16 = jnp.bfloat16
LANES = 128
CHUNK_LO = 512
CHUNK_HI = 640
PACKED = 768


def swiglu_parts(gate_value, up_value):
    gate_float = gate_value.astype(F32)
    up_float = up_value.astype(F32)
    sigmoid_gate = jax.nn.sigmoid(gate_float)
    activated = gate_float * sigmoid_gate
    hidden_state = (activated * up_float).astype(BF16)
    gate_factor = up_float * sigmoid_gate * (1.0 + gate_float * (1.0 - sigmoid_gate))
    return (hidden_state, gate_factor, activated)


def whole(count):
    return [pl.BlockSpec(memory_space=pltpu.VMEM)] * count


def pack_kernel(cot_ref, routed_ref, shared_ref, out_ref):
    n_tensor = out_ref.shape[0] // 8
    width = cot_ref.shape[1] // n_tensor
    per_expert = routed_ref.shape[2] // LANES
    experts = routed_ref.shape[0]
    cot = cot_ref[...].astype(F32)

    def chunk(t):
        if t < experts * per_expert:
            column = t % per_expert * LANES
            return routed_ref[t // per_expert, :, column : column + LANES].astype(F32)
        if t == experts * per_expert:
            return shared_ref[...].astype(F32)
        return jnp.zeros((16, LANES), F32)

    for pair in range(n_tensor // 2):
        even, odd = 2 * pair, 2 * pair + 1
        rows = pl.ds(16 * pair, 16)
        tokens = jnp.concatenate(
            [cot[:, even * width : (even + 1) * width], cot[:, odd * width : (odd + 1) * width]],
            axis=0,
        )
        out_ref[rows, 0:width] = tokens.astype(BF16)
        out_ref[rows, width:CHUNK_LO] = jnp.zeros((16, CHUNK_LO - width), BF16)
        first, second = chunk(even), chunk(odd)
        out_ref[rows, CHUNK_LO:CHUNK_HI] = jnp.concatenate([first[0:8], second[0:8]], 0).astype(BF16)
        out_ref[rows, CHUNK_HI:PACKED] = jnp.concatenate([first[8:16], second[8:16]], 0).astype(BF16)


def dispatch_kernel(index_ref, weight_ref, packed_ref, out_ref, columns_ref, chunk_ref):
    tokens = packed_ref.shape[0]
    width = out_ref.shape[1]
    top = index_ref.shape[0]
    peers = out_ref.shape[0] // 24
    columns = packed_ref[:, 0:width]
    columns_ref[...] = columns
    for half, lane in enumerate((CHUNK_LO, CHUNK_HI)):
        partial = packed_ref[:, lane : lane + LANES].astype(F32).reshape(tokens // 8, 8, LANES)
        chunk_ref[8 * half : 8 * half + 8, :] = jnp.sum(partial, axis=0)
    before = (
        lax.broadcasted_iota(jnp.int32, (tokens, tokens), 0)
        < lax.broadcasted_iota(jnp.int32, (tokens, tokens), 1)
    ).astype(BF16)
    weights, slots = [], []
    for local in range(2):
        expert = 2 * lax.broadcasted_iota(jnp.int32, (peers, tokens), 0) + local
        weight = jnp.zeros((peers, tokens), F32)
        named = jnp.zeros((peers, tokens), F32)
        for k in range(top):
            match = expert == index_ref[k : k + 1, :]
            weight = jnp.where(match, weight_ref[k : k + 1, :], weight)
            named = jnp.where(match, 1.0, named)
        slot = jnp.dot(named.astype(BF16), before, preferred_element_type=F32)
        weights.append(weight)
        slots.append(slot)
    row = lax.broadcasted_iota(jnp.int32, (peers, 24, tokens), 1)
    first = row < 12
    wanted = jnp.where(first, row, row - 12).astype(F32)
    shape = (peers, 24, tokens)
    slot = jnp.where(
        first,
        jnp.broadcast_to(slots[0][:, None, :], shape),
        jnp.broadcast_to(slots[1][:, None, :], shape),
    )
    weight = jnp.where(
        first,
        jnp.broadcast_to(weights[0][:, None, :], shape),
        jnp.broadcast_to(weights[1][:, None, :], shape),
    )
    selector = jnp.where(slot == wanted, weight, 0.0).reshape(peers * 24, tokens)
    high = selector.astype(BF16)
    low = (selector - high.astype(F32)).astype(BF16)
    left = jnp.concatenate([high, low], axis=1)
    right = jnp.concatenate([columns, columns], axis=0)
    out_ref[...] = jnp.dot(left, right, preferred_element_type=F32).astype(BF16)


def routed_kernel(arrived_ref, weight_ref, map_ref, chunk_ref, part_ref, rows_ref, gather_ref, held):
    local, step = pl.program_id(0), pl.program_id(1)
    slots = rows_ref.shape[1]
    block = 192

    @pl.when(step == 0)
    def _():
        i = lax.broadcasted_iota(jnp.int32, (block, 2 * block), 0)
        j = lax.broadcasted_iota(jnp.int32, (block, 2 * block), 1)
        group = lax.shift_right_logical(i * 5462, 16)
        pick = (j - i == 12 * (group + local)).astype(BF16)
        for b in range(slots // block):
            rows = jnp.dot(
                pick,
                arrived_ref[2 * block * b : 2 * block * (b + 1), :],
                preferred_element_type=F32,
            ).astype(BF16)
            held[block * b : block * (b + 1), :] = rows
        rows_ref[0] = held[...]
        rank = lax.dot_general(
            map_ref[0], held[...], (((1,), (1,)), ((), ())), preferred_element_type=F32
        ).astype(BF16)

        @pl.when(local == 0)
        def _():
            gather_ref[:, 0:slots] = rank
            gather_ref[:, 2 * slots : 2 * slots + LANES] = chunk_ref[...].astype(BF16)

        @pl.when(local == 1)
        def _():
            gather_ref[:, slots : 2 * slots] = rank

    part = lax.dot_general(
        weight_ref[0], held[...], (((0,), (1,)), ((), ())), preferred_element_type=F32
    ).astype(BF16)
    part_ref[...] = part.reshape(part_ref.shape)


def shards(
    cotangent,
    routed_expert_index,
    chosen_gate_weight,
    routed_down_weight,
    routed_adapter_input_map,
    routed_adapter_output_map,
    routed_gate_saved,
    routed_up_saved,
    shared_down_weight,
    shared_adapter_input_map,
    shared_adapter_output_map,
    shared_gate_saved,
    shared_up_saved,
):
    n_tensor = lax.axis_size("tensor")
    group_count = lax.axis_size("expert") * lax.axis_size("dp")
    expert_local, expert_hidden, width = routed_down_weight.shape
    hidden_local = expert_hidden // n_tensor
    slot_count = routed_gate_saved.shape[2]
    rank_size = routed_adapter_output_map.shape[1]
    scale = ADAPTER_SCALE / group_count
    contract_trailing = (((1,), (1,)), ((), ()))
    contract_first = (((0,), (0,)), ((), ()))

    token_rows = lax.all_gather(cotangent, "tensor", axis=1, tiled=True)[0]
    tokens = token_rows.shape[0]

    routed_hidden, routed_gate_factor, routed_activated = swiglu_parts(
        routed_gate_saved, routed_up_saved
    )
    shared_hidden, shared_gate_factor, shared_activated = swiglu_parts(
        shared_gate_saved[0], shared_up_saved[0]
    )
    routed_inner_part = jnp.einsum(
        "fes,efr->ers", routed_hidden, routed_adapter_input_map, preferred_element_type=F32
    ).astype(BF16)
    shared_inner_part = lax.dot_general(
        shared_adapter_input_map,
        shared_hidden,
        (((0,), (1,)), ((), ())),
        preferred_element_type=F32,
    ).astype(BF16)
    packed = pl.pallas_call(
        pack_kernel,
        out_shape=jax.ShapeDtypeStruct((8 * n_tensor, PACKED), BF16),
        in_specs=whole(3),
        out_specs=whole(1)[0],
        name="pack",
    )(cotangent[0], routed_inner_part, shared_inner_part)
    packed = lax.all_to_all(packed, "tensor", split_axis=0, concat_axis=0, tiled=True)

    outgoing, own_columns, inner_chunk = pl.pallas_call(
        dispatch_kernel,
        out_shape=(
            jax.ShapeDtypeStruct((group_count * 24, width), BF16),
            jax.ShapeDtypeStruct((tokens, width), BF16),
            jax.ShapeDtypeStruct((rank_size, LANES), F32),
        ),
        in_specs=whole(3),
        out_specs=tuple(whole(3)),
        name="dispatch",
        compiler_params=pltpu.CompilerParams(vmem_limit_bytes=32 * 1024 * 1024),
    )(routed_expert_index[0].T, chosen_gate_weight[0].T, packed)
    arrived = lax.all_to_all(
        outgoing.reshape(group_count, 24, width),
        ("expert", "dp"),
        split_axis=0,
        concat_axis=0,
        tiled=True,
    ).reshape(group_count * 24, width)

    steps = 4
    fan = n_tensor // steps
    part, routed_rows, rank_part = pl.pallas_call(
        routed_kernel,
        grid=(expert_local, steps),
        out_shape=(
            jax.ShapeDtypeStruct((n_tensor, expert_local, hidden_local, slot_count), BF16),
            jax.ShapeDtypeStruct((expert_local, slot_count, width), BF16),
            jax.ShapeDtypeStruct((rank_size, expert_local * slot_count + LANES), BF16),
        ),
        in_specs=[
            pl.BlockSpec((group_count * 24, width), lambda e, j: (0, 0)),
            pl.BlockSpec((1, width, expert_hidden // steps), lambda e, j: (e, 0, j)),
            pl.BlockSpec((1, rank_size, width), lambda e, j: (e, 0, 0)),
            pl.BlockSpec((rank_size, LANES), lambda e, j: (0, 0)),
        ],
        out_specs=(
            pl.BlockSpec((fan, 1, hidden_local, slot_count), lambda e, j: (j, e, 0, 0)),
            pl.BlockSpec((1, slot_count, width), lambda e, j: (e, 0, 0)),
            pl.BlockSpec((rank_size, expert_local * slot_count + LANES), lambda e, j: (0, 0)),
        ),
        scratch_shapes=[pltpu.VMEM((slot_count, width), BF16)],
        name="routed",
        compiler_params=pltpu.CompilerParams(vmem_limit_bytes=48 * 1024 * 1024),
    )(
        arrived,
        jnp.swapaxes(routed_down_weight, 1, 2),
        routed_adapter_output_map,
        inner_chunk,
    )
    part, rank_part, token_rows = lax.optimization_barrier((part, rank_part, token_rows))
    hidden_gradient = lax.psum_scatter(
        part.reshape(n_tensor * expert_local * hidden_local, slot_count),
        "tensor",
        scatter_dimension=0,
        tiled=True,
    ).reshape(expert_local, hidden_local, slot_count)

    gathered = lax.all_gather(rank_part, "tensor", axis=0, tiled=True).reshape(
        n_tensor, rank_size, -1
    )
    edge = expert_local * slot_count
    routed_rank = jnp.sum(gathered[:, :, :edge].astype(F32), axis=0).astype(BF16)
    routed_rank = jnp.swapaxes(routed_rank.reshape(rank_size, expert_local, slot_count), 0, 1)
    inner_chunks = gathered[:, :, edge:]
    n_chunks = edge // LANES
    routed_inner = (
        inner_chunks[:n_chunks]
        .reshape(expert_local, n_chunks // expert_local, rank_size, LANES)
        .transpose(0, 2, 1, 3)
        .reshape(expert_local, rank_size, slot_count)
    )
    shared_inner = inner_chunks[n_chunks]

    shared_rank = lax.dot_general(
        token_rows, shared_adapter_output_map, contract_trailing, preferred_element_type=F32
    ).astype(BF16)
    adapter_a = lax.dot_general(
        shared_rank, shared_hidden, contract_first, preferred_element_type=F32
    )
    adapter_b = jnp.dot(shared_inner, own_columns, preferred_element_type=F32)
    adapter = jnp.concatenate([adapter_a, adapter_b], axis=1)
    adapter = jnp.sum(lax.all_gather(adapter, "dp"), axis=0)
    adapter = scale * jnp.sum(lax.all_gather(adapter, "expert"), axis=0)
    grad_a_shared = adapter[:, : adapter_a.shape[1]].T
    grad_b_shared = adapter[:, adapter_a.shape[1] :]

    shared_gradient = lax.dot_general(
        token_rows, shared_down_weight, contract_trailing, preferred_element_type=F32
    )
    shared_gradient = shared_gradient + ADAPTER_SCALE * lax.dot_general(
        shared_rank, shared_adapter_input_map, contract_trailing, preferred_element_type=F32
    )
    grad_gate_shared = (shared_gradient * shared_gate_factor).astype(BF16)[None]
    grad_up_shared = (shared_gradient * shared_activated).astype(BF16)[None]

    grad_a_routed = scale * jnp.einsum(
        "fes,ers->efr", routed_hidden, routed_rank, preferred_element_type=F32
    )
    grad_b_routed = scale * jnp.einsum(
        "ers,esd->erd", routed_inner, routed_rows, preferred_element_type=F32
    )
    low_rank = ADAPTER_SCALE * jnp.einsum(
        "ers,efr->efs", routed_rank, routed_adapter_input_map, preferred_element_type=F32
    )
    hidden_gradient = jnp.swapaxes(hidden_gradient.astype(F32) + low_rank, 0, 1)
    grad_gate_routed = (hidden_gradient * routed_gate_factor).astype(BF16)
    grad_up_routed = (hidden_gradient * routed_activated).astype(BF16)
    return (
        grad_gate_routed,
        grad_up_routed,
        grad_gate_shared,
        grad_up_shared,
        grad_a_routed,
        grad_b_routed,
        grad_a_shared,
        grad_b_shared,
    )


def solution(mesh):
    placed = (
        P(("expert", "dp"), "tensor", None),
        P(("expert", "dp"), None, None),
        P(("expert", "dp"), None, None),
        P(("expert", "dp"), None, "tensor"),
        P(("expert", "dp"), "tensor", None),
        P(("expert", "dp"), None, "tensor"),
        P("tensor", ("expert", "dp"), None),
        P("tensor", ("expert", "dp"), None),
        P("tensor", None),
        P("tensor", None),
        P(),
        P(("expert", "dp"), None, "tensor"),
        P(("expert", "dp"), None, "tensor"),
    )
    return jax.shard_map(
        shards,
        mesh=mesh,
        in_specs=placed,
        out_specs=(
            P("tensor", ("expert", "dp"), None),
            P("tensor", ("expert", "dp"), None),
            P(("expert", "dp"), None, "tensor"),
            P(("expert", "dp"), None, "tensor"),
            P(("expert", "dp"), "tensor", None),
            P(("expert", "dp"), None, "tensor"),
            P("tensor", None),
            P(None, "tensor"),
        ),
        check_vma=False,
    )
```

```python
import jax
import jax.numpy as jnp
from jax import lax
from jax.experimental import pallas as pl
from jax.experimental.pallas import tpu as pltpu
from jax.sharding import PartitionSpec as P

ADAPTER_SCALE = 2.0
F32 = jnp.float32
BF16 = jnp.bfloat16
LANES = 128


def swiglu_parts(gate_value, up_value):
    gate_float = gate_value.astype(F32)
    up_float = up_value.astype(F32)
    sigmoid_gate = jax.nn.sigmoid(gate_float)
    activated = gate_float * sigmoid_gate
    hidden_state = (activated * up_float).astype(BF16)
    gate_factor = up_float * sigmoid_gate * (1.0 + gate_float * (1.0 - sigmoid_gate))
    return (hidden_state, gate_factor, activated)


def whole(count):
    return [pl.BlockSpec(memory_space=pltpu.VMEM)] * count


def pack_kernel(cot_ref, routed_ref, shared_ref, map_ref, out_ref):
    n_tensor = out_ref.shape[0] // 8
    width = cot_ref.shape[1] // n_tensor
    per_expert = routed_ref.shape[2] // LANES
    experts = routed_ref.shape[0]

    def chunk(t):
        if t < experts * per_expert:
            column = t % per_expert * LANES
            return routed_ref[t // per_expert, :, column : column + LANES].astype(F32)
        return jnp.zeros((16, LANES), F32)

    rank = lax.dot_general(
        cot_ref[...], map_ref[...], (((1,), (1,)), ((), ())), preferred_element_type=F32
    )
    rank = jnp.concatenate([rank, jnp.zeros((8, LANES - rank.shape[1]), F32)], axis=1)
    shared = shared_ref[...].astype(F32)
    common = [shared[0:8], shared[8:16], rank]
    common = [jnp.concatenate([x, x], axis=0).astype(BF16) for x in common]

    for pair in range(n_tensor // 2):
        rows = pl.ds(16 * pair, 16)
        both = cot_ref[:, 2 * pair * width : 2 * (pair + 1) * width].astype(F32)
        swapped = jnp.concatenate([both[:, width:], both[:, :width]], axis=1)
        out_ref[rows, 0 : 2 * width] = jnp.concatenate([both, swapped], axis=0).astype(BF16)
        first, second = chunk(2 * pair), chunk(2 * pair + 1)
        low = jnp.concatenate([first[0:8], second[0:8]], axis=0)
        high = jnp.concatenate([first[8:16], second[8:16]], axis=0)
        out_ref[rows, 2 * width : 2 * width + LANES] = low.astype(BF16)
        out_ref[rows, 2 * width + LANES : 2 * width + 2 * LANES] = high.astype(BF16)
        for n, x in enumerate(common):
            lane = 2 * width + (2 + n) * LANES
            out_ref[rows, lane : lane + LANES] = x


def dispatch_kernel(
    parity_ref,
    index_ref,
    weight_ref,
    packed_ref,
    hidden_ref,
    out_ref,
    chunk_ref,
    rank_ref,
    adapter_ref,
):
    tokens = packed_ref.shape[0]
    width = adapter_ref.shape[1] - hidden_ref.shape[1]
    top = index_ref.shape[0]
    peers = out_ref.shape[0] // 8
    own = packed_ref[:, 0:width]
    other = packed_ref[:, width : 2 * width]

    def summed(lane):
        halves = []
        for first in (lane, lane + LANES):
            partial = packed_ref[:, first : first + LANES].astype(F32)
            halves.append(jnp.sum(partial.reshape(tokens // 8, 8, LANES), axis=0))
        return jnp.concatenate(halves, axis=0).astype(BF16)

    chunk_ref[...] = summed(2 * width)
    shared_inner = summed(2 * width + 2 * LANES)
    shared_rank = packed_ref[:, 2 * width + 4 * LANES : 2 * width + 5 * LANES]
    rank_ref[...] = shared_rank
    adapter_a = lax.dot_general(
        shared_rank, hidden_ref[...], (((0,), (0,)), ((), ())), preferred_element_type=F32
    )
    adapter_ref[:, 0 : hidden_ref.shape[1]] = adapter_a[0 : adapter_ref.shape[0]]
    adapter_ref[:, hidden_ref.shape[1] :] = jnp.dot(
        shared_inner, own, preferred_element_type=F32
    )
    before = (
        lax.broadcasted_iota(jnp.int32, (tokens, tokens), 0)
        < lax.broadcasted_iota(jnp.int32, (tokens, tokens), 1)
    ).astype(BF16)
    expert = 2 * lax.broadcasted_iota(jnp.int32, (peers, tokens), 0) + parity_ref[0]
    weight = jnp.zeros((peers, tokens), F32)
    named = jnp.zeros((peers, tokens), F32)
    for k in range(top):
        match = expert == index_ref[k : k + 1, :]
        weight = jnp.where(match, weight_ref[k : k + 1, :], weight)
        named = jnp.where(match, 1.0, named)
    slot = jnp.dot(named.astype(BF16), before, preferred_element_type=F32)
    shape = (peers, 8, tokens)
    row = lax.broadcasted_iota(jnp.int32, shape, 1)
    slot = jnp.broadcast_to(slot[:, None, :], shape)
    weight = jnp.broadcast_to(weight[:, None, :], shape)

    def split(selector):
        selector = selector.reshape(peers * 8, tokens)
        high = selector.astype(BF16)
        return high, (selector - high.astype(F32)).astype(BF16)

    high, low = split(jnp.where(slot == row.astype(F32), weight, 0.0))
    left = jnp.concatenate([high, low], axis=1)
    both = packed_ref[:, 0 : 2 * width]
    right = jnp.concatenate([both, both], axis=0)
    out_ref[:, 0 : 2 * width] = jnp.dot(left, right, preferred_element_type=F32).astype(BF16)
    wanted = jnp.where(row < 4, row + 8, row + 4).astype(F32)
    tail = jnp.where(slot == wanted, weight, 0.0)
    first = split(jnp.where(row < 4, tail, 0.0))
    second = split(jnp.where(row < 4, 0.0, tail))
    left = jnp.concatenate([first[0], first[1], second[0], second[1]], axis=1)
    right = jnp.concatenate([own, own, other, other], axis=0)
    out_ref[:, 2 * width : 3 * width] = jnp.dot(left, right, preferred_element_type=F32).astype(BF16)
    rest = out_ref.shape[1] - 3 * width
    out_ref[:, 3 * width :] = jnp.zeros((peers * 8, rest), BF16)


def routed_kernel(
    parity_ref,
    arrived_ref,
    own_weight_ref,
    pair_weight_ref,
    own_map_ref,
    pair_map_ref,
    chunk_ref,
    part_ref,
    own_rows_ref,
    pair_rows_ref,
    gather_ref,
):
    del parity_ref
    slots, width = own_rows_ref.shape
    block, groups = 192, 16
    turned = (((0,), (1,)), ((), ()))

    @pl.when(pl.program_id(0) == 0)
    def _():
        i = lax.broadcasted_iota(jnp.int32, (block, 8 * groups), 0)
        j = lax.broadcasted_iota(jnp.int32, (block, 8 * groups), 1)
        group = lax.shift_right_logical(i * 5462, 16)
        slot = i - 12 * group
        head = (j == 8 * group + slot) & (slot < 8)
        for half, rows_ref in enumerate((own_rows_ref, pair_rows_ref)):
            tail = (j == 8 * group + slot - 8 + 4 * half) & (slot >= 8)
            pick = jnp.concatenate([head.astype(F32), tail.astype(F32)], axis=1).astype(BF16)
            for b in range(slots // block):
                rows = pl.ds(8 * groups * b, 8 * groups)
                source = jnp.concatenate(
                    [
                        arrived_ref[rows, half * width : (half + 1) * width],
                        arrived_ref[rows, 2 * width : 3 * width],
                    ],
                    axis=0,
                )
                rows_ref[block * b : block * (b + 1), :] = jnp.dot(
                    pick, source, preferred_element_type=F32
                ).astype(BF16)
        rank = lax.dot_general(
            own_map_ref[0], own_rows_ref[...], (((1,), (1,)), ((), ())), preferred_element_type=F32
        )
        pair_rank = lax.dot_general(
            pair_map_ref[...], pair_rows_ref[...], turned, preferred_element_type=F32
        )
        gather_ref[:, 0:slots] = (rank + pair_rank[0 : rank.shape[0]]).astype(BF16)
        gather_ref[:, slots : slots + LANES] = chunk_ref[...]

    part = lax.dot_general(
        own_weight_ref[0], own_rows_ref[...], turned, preferred_element_type=F32
    ) + lax.dot_general(
        pair_weight_ref[...], pair_rows_ref[...], turned, preferred_element_type=F32
    )
    part_ref[...] = part.astype(BF16)


def shards(
    cotangent,
    routed_expert_index,
    chosen_gate_weight,
    routed_down_weight,
    routed_adapter_input_map,
    routed_adapter_output_map,
    routed_gate_saved,
    routed_up_saved,
    shared_down_weight,
    shared_adapter_input_map,
    shared_adapter_output_map,
    shared_gate_saved,
    shared_up_saved,
):
    n_tensor = lax.axis_size("tensor")
    group_count = lax.axis_size("expert") * lax.axis_size("dp")
    expert_local, expert_hidden, width = routed_down_weight.shape
    hidden_local = expert_hidden // n_tensor
    slot_count = routed_gate_saved.shape[2]
    rank_size = routed_adapter_output_map.shape[1]
    scale = ADAPTER_SCALE / group_count
    contract_trailing = (((1,), (1,)), ((), ()))
    parity = lax.bitwise_and(lax.axis_index("tensor"), 1)
    even = parity == 0
    parity_scalar = parity.reshape(1)
    swap = [(t, t ^ 1) for t in range(n_tensor)]
    same_parity = [list(range(p, n_tensor, 2)) for p in range(2)]

    def pick(array, index, size):
        return lax.dynamic_slice_in_dim(array, index * size, size, 0, allow_negative_indices=False)

    token_rows = lax.all_gather(cotangent, "tensor", axis=1, tiled=True)[0]
    tokens = token_rows.shape[0]

    routed_hidden, routed_gate_factor, routed_activated = swiglu_parts(
        routed_gate_saved, routed_up_saved
    )
    shared_hidden, shared_gate_factor, shared_activated = swiglu_parts(
        shared_gate_saved[0], shared_up_saved[0]
    )
    routed_inner_part = jnp.einsum(
        "fes,efr->ers", routed_hidden, routed_adapter_input_map, preferred_element_type=F32
    ).astype(BF16)
    shared_inner_part = lax.dot_general(
        shared_adapter_input_map,
        shared_hidden,
        (((0,), (1,)), ((), ())),
        preferred_element_type=F32,
    ).astype(BF16)
    packed = pl.pallas_call(
        pack_kernel,
        out_shape=jax.ShapeDtypeStruct((8 * n_tensor, 2 * width + 5 * LANES), BF16),
        in_specs=whole(4),
        out_specs=whole(1)[0],
        name="pack",
    )(cotangent[0], routed_inner_part, shared_inner_part, shared_adapter_output_map)
    packed = lax.all_to_all(packed, "tensor", split_axis=0, concat_axis=0, tiled=True)

    block_width = -(-3 * width // LANES) * LANES
    shared_local = shared_hidden.shape[1]
    outgoing, inner_chunk, shared_rank, adapter = pl.pallas_call(
        dispatch_kernel,
        out_shape=(
            jax.ShapeDtypeStruct((group_count * 8, block_width), BF16),
            jax.ShapeDtypeStruct((rank_size, LANES), BF16),
            jax.ShapeDtypeStruct((tokens, LANES), BF16),
            jax.ShapeDtypeStruct((rank_size, shared_local + width), F32),
        ),
        in_specs=[pl.BlockSpec(memory_space=pltpu.SMEM)] + whole(4),
        out_specs=tuple(whole(4)),
        name="dispatch",
        compiler_params=pltpu.CompilerParams(vmem_limit_bytes=32 * 1024 * 1024),
    )(parity_scalar, routed_expert_index[0].T, chosen_gate_weight[0].T, packed, shared_hidden)
    shared_rank = shared_rank[:, :rank_size]

    sent_weight = jnp.concatenate(
        [
            pick(routed_down_weight, 1 - parity, 1)[0],
            pick(routed_adapter_output_map, 1 - parity, 1)[0],
            jnp.zeros((LANES - rank_size, width), BF16),
        ],
        axis=0,
    ).T
    outgoing, sent_weight = lax.optimization_barrier((outgoing, sent_weight))
    pair_weight = lax.ppermute(sent_weight, "tensor", swap)
    arrived = lax.all_to_all(
        outgoing, ("expert", "dp"), split_axis=0, concat_axis=0, tiled=True
    )
    adapter = jnp.sum(lax.all_gather(adapter, "dp"), axis=0)
    adapter = scale * jnp.sum(lax.all_gather(adapter, "expert"), axis=0)
    arrived, adapter = lax.optimization_barrier((arrived, adapter))
    grad_a_shared = adapter[:, :shared_local].T
    grad_b_shared = adapter[:, shared_local:]

    steps = 4
    fan = expert_hidden // steps
    part, own_rows, pair_rows, rank_part = pl.pallas_call(
        routed_kernel,
        grid_spec=pltpu.PrefetchScalarGridSpec(
            num_scalar_prefetch=1,
            grid=(steps,),
            in_specs=[
                pl.BlockSpec((group_count * 8, block_width), lambda j, p: (0, 0)),
                pl.BlockSpec((1, width, fan), lambda j, p: (p[0], 0, j)),
                pl.BlockSpec((width, fan), lambda j, p: (0, j)),
                pl.BlockSpec((1, rank_size, width), lambda j, p: (p[0], 0, 0)),
                pl.BlockSpec((width, LANES), lambda j, p: (0, expert_hidden // LANES)),
                pl.BlockSpec((rank_size, LANES), lambda j, p: (0, 0)),
            ],
            out_specs=(
                pl.BlockSpec((fan, slot_count), lambda j, p: (j, 0)),
                pl.BlockSpec((slot_count, width), lambda j, p: (0, 0)),
                pl.BlockSpec((slot_count, width), lambda j, p: (0, 0)),
                pl.BlockSpec((rank_size, slot_count + LANES), lambda j, p: (0, 0)),
            ),
        ),
        out_shape=(
            jax.ShapeDtypeStruct((expert_hidden, slot_count), BF16),
            jax.ShapeDtypeStruct((slot_count, width), BF16),
            jax.ShapeDtypeStruct((slot_count, width), BF16),
            jax.ShapeDtypeStruct((rank_size, slot_count + LANES), BF16),
        ),
        name="routed",
        compiler_params=pltpu.CompilerParams(vmem_limit_bytes=48 * 1024 * 1024),
    )(
        parity_scalar,
        arrived,
        jnp.swapaxes(routed_down_weight, 1, 2),
        pair_weight,
        routed_adapter_output_map,
        pair_weight,
        inner_chunk,
    )
    part, rank_part, token_rows = lax.optimization_barrier((part, rank_part, token_rows))
    reduced = lax.psum_scatter(
        part, "tensor", scatter_dimension=0, axis_index_groups=same_parity, tiled=True
    )
    kept = pick(reduced, parity, hidden_local)
    given = pick(reduced, 1 - parity, hidden_local)
    taken = lax.ppermute(given, "tensor", swap)
    hidden_gradient = jnp.stack(
        [jnp.where(even, kept, taken), jnp.where(even, taken, kept)], axis=1
    )

    gathered = lax.all_gather(rank_part, "tensor", axis=0, tiled=True).reshape(
        n_tensor, rank_size, -1
    )
    routed_rank = jnp.sum(
        gathered[:, :, :slot_count]
        .reshape(n_tensor // 2, expert_local, rank_size, slot_count)
        .astype(F32),
        axis=0,
    ).astype(BF16)
    chunks = slot_count // LANES
    inner_chunks = gathered[:, :, slot_count:]
    own_inner = pick(inner_chunks, parity, chunks)
    own_inner = jnp.swapaxes(own_inner, 0, 1).reshape(rank_size, slot_count)
    shared_gradient = lax.dot_general(
        token_rows, shared_down_weight, contract_trailing, preferred_element_type=F32
    )
    shared_gradient = shared_gradient + ADAPTER_SCALE * lax.dot_general(
        shared_rank, shared_adapter_input_map, contract_trailing, preferred_element_type=F32
    )
    grad_gate_shared = (shared_gradient * shared_gate_factor).astype(BF16)[None]
    grad_up_shared = (shared_gradient * shared_activated).astype(BF16)[None]

    grad_a_routed = scale * jnp.einsum(
        "fes,ers->efr", routed_hidden, routed_rank, preferred_element_type=F32
    )
    own_b = scale * jnp.dot(own_inner, own_rows, preferred_element_type=F32)
    pair_b = scale * jnp.dot(own_inner, pair_rows, preferred_element_type=F32)
    pair_b = lax.ppermute(pair_b, "tensor", swap)
    grad_b_routed = jnp.stack([jnp.where(even, own_b, pair_b), jnp.where(even, pair_b, own_b)])
    low_rank = ADAPTER_SCALE * jnp.einsum(
        "ers,efr->fes", routed_rank, routed_adapter_input_map, preferred_element_type=F32
    )
    hidden_gradient = hidden_gradient.astype(F32) + low_rank
    grad_gate_routed = (hidden_gradient * routed_gate_factor).astype(BF16)
    grad_up_routed = (hidden_gradient * routed_activated).astype(BF16)
    return (
        grad_gate_routed,
        grad_up_routed,
        grad_gate_shared,
        grad_up_shared,
        grad_a_routed,
        grad_b_routed,
        grad_a_shared,
        grad_b_shared,
    )


def solution(mesh):
    placed = (
        P(("expert", "dp"), "tensor", None),
        P(("expert", "dp"), None, None),
        P(("expert", "dp"), None, None),
        P(("expert", "dp"), None, "tensor"),
        P(("expert", "dp"), "tensor", None),
        P(("expert", "dp"), None, "tensor"),
        P("tensor", ("expert", "dp"), None),
        P("tensor", ("expert", "dp"), None),
        P("tensor", None),
        P("tensor", None),
        P(),
        P(("expert", "dp"), None, "tensor"),
        P(("expert", "dp"), None, "tensor"),
    )
    return jax.shard_map(
        shards,
        mesh=mesh,
        in_specs=placed,
        out_specs=(
            P("tensor", ("expert", "dp"), None),
            P("tensor", ("expert", "dp"), None),
            P(("expert", "dp"), None, "tensor"),
            P(("expert", "dp"), None, "tensor"),
            P(("expert", "dp"), "tensor", None),
            P(("expert", "dp"), None, "tensor"),
            P("tensor", None),
            P(None, "tensor"),
        ),
        check_vma=False,
    )
```

```python
import functools

import jax
import jax.numpy as jnp
from jax import lax
from jax.experimental import pallas as pl
from jax.experimental.pallas import tpu as pltpu
from jax.sharding import PartitionSpec as P

ADAPTER_SCALE = 2.0
F32 = jnp.float32
BF16 = jnp.bfloat16
LANES = 128


def swiglu_parts(gate_value, up_value):
    gate_float = gate_value.astype(F32)
    up_float = up_value.astype(F32)
    sigmoid_gate = jax.nn.sigmoid(gate_float)
    activated = gate_float * sigmoid_gate
    hidden_state = (activated * up_float).astype(BF16)
    gate_factor = up_float * sigmoid_gate * (1.0 + gate_float * (1.0 - sigmoid_gate))
    return (hidden_state, gate_factor, activated)


def whole(count):
    return [pl.BlockSpec(memory_space=pltpu.VMEM)] * count


def pack_kernel(
    cot_ref,
    routed_ref,
    routed_map_ref,
    gate_ref,
    up_ref,
    shared_map_ref,
    map_ref,
    out_ref,
    hidden_ref,
):
    n_tensor = out_ref.shape[0] // 8
    width = cot_ref.shape[1] // n_tensor
    per_expert = routed_ref.shape[2] // LANES
    experts = routed_ref.shape[0]
    inner = [
        jnp.dot(routed_map_ref[e], routed_ref[e], preferred_element_type=F32)
        for e in range(experts)
    ]
    hidden = swiglu_parts(gate_ref[...], up_ref[...])[0]
    hidden_ref[...] = hidden
    shared = lax.dot_general(
        shared_map_ref[...], hidden, (((1,), (1,)), ((), ())), preferred_element_type=F32
    )

    def chunk(t):
        if t < experts * per_expert:
            column = t % per_expert * LANES
            return inner[t // per_expert][:, column : column + LANES]
        return jnp.zeros((16, LANES), F32)

    rank = lax.dot_general(
        cot_ref[...], map_ref[...], (((1,), (1,)), ((), ())), preferred_element_type=F32
    )
    rank = jnp.concatenate([rank, jnp.zeros((8, LANES - rank.shape[1]), F32)], axis=1)
    common = [shared[0:8], shared[8:16], rank]
    common = [jnp.concatenate([x, x], axis=0).astype(BF16) for x in common]

    for pair in range(n_tensor // 2):
        rows = pl.ds(16 * pair, 16)
        both = cot_ref[:, 2 * pair * width : 2 * (pair + 1) * width].astype(F32)
        swapped = jnp.concatenate([both[:, width:], both[:, :width]], axis=1)
        out_ref[rows, 0 : 2 * width] = jnp.concatenate([both, swapped], axis=0).astype(BF16)
        first, second = chunk(2 * pair), chunk(2 * pair + 1)
        low = jnp.concatenate([first[0:8], second[0:8]], axis=0)
        high = jnp.concatenate([first[8:16], second[8:16]], axis=0)
        out_ref[rows, 2 * width : 2 * width + LANES] = low.astype(BF16)
        out_ref[rows, 2 * width + LANES : 2 * width + 2 * LANES] = high.astype(BF16)
        for n, x in enumerate(common):
            lane = 2 * width + (2 + n) * LANES
            out_ref[rows, lane : lane + LANES] = x


def dispatch_kernel(
    parity_ref,
    index_ref,
    weight_ref,
    packed_ref,
    hidden_ref,
    out_ref,
    chunk_ref,
    rank_ref,
    adapter_ref,
):
    tokens = packed_ref.shape[0]
    width = adapter_ref.shape[1] - hidden_ref.shape[1]
    top = index_ref.shape[0]
    peers = out_ref.shape[0] // 8
    own = packed_ref[:, 0:width]
    other = packed_ref[:, width : 2 * width]

    def summed(lane):
        halves = []
        for first in (lane, lane + LANES):
            partial = packed_ref[:, first : first + LANES].astype(F32)
            halves.append(jnp.sum(partial.reshape(tokens // 8, 8, LANES), axis=0))
        return jnp.concatenate(halves, axis=0).astype(BF16)

    chunk_ref[...] = summed(2 * width)
    shared_inner = summed(2 * width + 2 * LANES)
    shared_rank = packed_ref[:, 2 * width + 4 * LANES : 2 * width + 5 * LANES]
    rank_ref[...] = shared_rank
    adapter_a = lax.dot_general(
        shared_rank, hidden_ref[...], (((0,), (0,)), ((), ())), preferred_element_type=F32
    )
    adapter_ref[:, 0 : hidden_ref.shape[1]] = adapter_a[0 : adapter_ref.shape[0]]
    adapter_ref[:, hidden_ref.shape[1] :] = jnp.dot(
        shared_inner, own, preferred_element_type=F32
    )
    before = (
        lax.broadcasted_iota(jnp.int32, (tokens, tokens), 0)
        < lax.broadcasted_iota(jnp.int32, (tokens, tokens), 1)
    ).astype(BF16)
    expert = 2 * lax.broadcasted_iota(jnp.int32, (peers, tokens), 0) + parity_ref[0]
    weight = jnp.zeros((peers, tokens), F32)
    named = jnp.zeros((peers, tokens), F32)
    for k in range(top):
        match = expert == index_ref[k : k + 1, :]
        weight = jnp.where(match, weight_ref[k : k + 1, :], weight)
        named = jnp.where(match, 1.0, named)
    slot = jnp.dot(named.astype(BF16), before, preferred_element_type=F32)
    shape = (peers, 8, tokens)
    row = lax.broadcasted_iota(jnp.int32, shape, 1)
    slot = jnp.broadcast_to(slot[:, None, :], shape)
    weight = jnp.broadcast_to(weight[:, None, :], shape)

    def split(selector):
        selector = selector.reshape(peers * 8, tokens)
        high = selector.astype(BF16)
        return high, (selector - high.astype(F32)).astype(BF16)

    high, low = split(jnp.where(slot == row.astype(F32), weight, 0.0))
    left = jnp.concatenate([high, low], axis=1)
    both = packed_ref[:, 0 : 2 * width]
    right = jnp.concatenate([both, both], axis=0)
    out_ref[:, 0 : 2 * width] = jnp.dot(left, right, preferred_element_type=F32).astype(BF16)
    wanted = jnp.where(row < 4, row + 8, row + 4).astype(F32)
    tail = jnp.where(slot == wanted, weight, 0.0)
    first = split(jnp.where(row < 4, tail, 0.0))
    second = split(jnp.where(row < 4, 0.0, tail))
    left = jnp.concatenate([first[0], first[1], second[0], second[1]], axis=1)
    right = jnp.concatenate([own, own, other, other], axis=0)
    out_ref[:, 2 * width : 3 * width] = jnp.dot(left, right, preferred_element_type=F32).astype(BF16)
    rest = out_ref.shape[1] - 3 * width
    out_ref[:, 3 * width :] = jnp.zeros((peers * 8, rest), BF16)


def routed_kernel(
    hidden_local,
    parity_ref,
    arrived_ref,
    own_weight_ref,
    pair_weight_ref,
    own_map_ref,
    pair_map_ref,
    chunk_ref,
    part_ref,
    own_rows_ref,
    pair_rows_ref,
    gather_ref,
):
    slots, width = own_rows_ref.shape
    block, groups = 192, 16
    turned = (((0,), (1,)), ((), ()))

    @pl.when(pl.program_id(0) == 0)
    def _():
        i = lax.broadcasted_iota(jnp.int32, (block, 8 * groups), 0)
        j = lax.broadcasted_iota(jnp.int32, (block, 8 * groups), 1)
        group = lax.shift_right_logical(i * 5462, 16)
        slot = i - 12 * group
        head = (j == 8 * group + slot) & (slot < 8)
        for half, rows_ref in enumerate((own_rows_ref, pair_rows_ref)):
            tail = (j == 8 * group + slot - 8 + 4 * half) & (slot >= 8)
            pick = jnp.concatenate([head.astype(F32), tail.astype(F32)], axis=1).astype(BF16)
            for b in range(slots // block):
                rows = pl.ds(8 * groups * b, 8 * groups)
                source = jnp.concatenate(
                    [
                        arrived_ref[rows, half * width : (half + 1) * width],
                        arrived_ref[rows, 2 * width : 3 * width],
                    ],
                    axis=0,
                )
                rows_ref[block * b : block * (b + 1), :] = jnp.dot(
                    pick, source, preferred_element_type=F32
                ).astype(BF16)
        rank = lax.dot_general(
            own_map_ref[0], own_rows_ref[...], (((1,), (1,)), ((), ())), preferred_element_type=F32
        )
        pair_rank = lax.dot_general(
            pair_map_ref[...], pair_rows_ref[...], turned, preferred_element_type=F32
        )
        gather_ref[:, 0:slots] = (rank + pair_rank[0 : rank.shape[0]]).astype(BF16)
        gather_ref[:, slots : slots + LANES] = chunk_ref[...]

    part = lax.dot_general(
        own_weight_ref[0], own_rows_ref[...], turned, preferred_element_type=F32
    ) + lax.dot_general(
        pair_weight_ref[...], pair_rows_ref[...], turned, preferred_element_type=F32
    )
    flip = 1 - parity_ref[0]
    for b in range(part.shape[0] // hidden_local):
        start = pl.multiple_of((b ^ flip) * hidden_local, hidden_local)
        part_ref[pl.ds(start, hidden_local), :] = part[
            b * hidden_local : (b + 1) * hidden_local
        ].astype(BF16)


def shards(
    cotangent,
    routed_expert_index,
    chosen_gate_weight,
    routed_down_weight,
    routed_adapter_input_map,
    routed_adapter_output_map,
    routed_gate_saved,
    routed_up_saved,
    shared_down_weight,
    shared_adapter_input_map,
    shared_adapter_output_map,
    shared_gate_saved,
    shared_up_saved,
):
    n_tensor = lax.axis_size("tensor")
    group_count = lax.axis_size("expert") * lax.axis_size("dp")
    expert_local, expert_hidden, width = routed_down_weight.shape
    hidden_local = expert_hidden // n_tensor
    slot_count = routed_gate_saved.shape[2]
    rank_size = routed_adapter_output_map.shape[1]
    scale = ADAPTER_SCALE / group_count
    contract_trailing = (((1,), (1,)), ((), ()))
    parity = lax.bitwise_and(lax.axis_index("tensor"), 1)
    even = parity == 0
    parity_scalar = parity.reshape(1)
    swap = [(t, t ^ 1) for t in range(n_tensor)]
    same_parity = [list(range(p, n_tensor, 2)) for p in range(2)]

    def pick(array, index, size):
        return lax.dynamic_slice_in_dim(array, index * size, size, 0, allow_negative_indices=False)

    token_rows = lax.all_gather(cotangent, "tensor", axis=1, tiled=True)[0]
    tokens = token_rows.shape[0]

    routed_hidden, routed_gate_factor, routed_activated = swiglu_parts(
        routed_gate_saved, routed_up_saved
    )
    shared_local = shared_gate_saved.shape[2]
    packed, shared_hidden = pl.pallas_call(
        pack_kernel,
        out_shape=(
            jax.ShapeDtypeStruct((8 * n_tensor, 2 * width + 5 * LANES), BF16),
            jax.ShapeDtypeStruct((tokens, shared_local), BF16),
        ),
        in_specs=whole(7),
        out_specs=tuple(whole(2)),
        name="pack",
    )(
        cotangent[0],
        jnp.swapaxes(routed_hidden, 0, 1),
        jnp.swapaxes(routed_adapter_input_map, 1, 2),
        shared_gate_saved[0],
        shared_up_saved[0],
        shared_adapter_input_map.T,
        shared_adapter_output_map,
    )
    packed = lax.all_to_all(packed, "tensor", split_axis=0, concat_axis=0, tiled=True)

    block_width = -(-3 * width // LANES) * LANES
    outgoing, inner_chunk, shared_rank, adapter = pl.pallas_call(
        dispatch_kernel,
        out_shape=(
            jax.ShapeDtypeStruct((group_count * 8, block_width), BF16),
            jax.ShapeDtypeStruct((rank_size, LANES), BF16),
            jax.ShapeDtypeStruct((tokens, LANES), BF16),
            jax.ShapeDtypeStruct((rank_size, shared_local + width), F32),
        ),
        in_specs=[pl.BlockSpec(memory_space=pltpu.SMEM)] + whole(4),
        out_specs=tuple(whole(4)),
        name="dispatch",
        compiler_params=pltpu.CompilerParams(vmem_limit_bytes=32 * 1024 * 1024),
    )(parity_scalar, routed_expert_index[0].T, chosen_gate_weight[0].T, packed, shared_hidden)
    shared_rank = shared_rank[:, :rank_size]

    sent_weight = jnp.concatenate(
        [
            pick(routed_down_weight, 1 - parity, 1)[0],
            pick(routed_adapter_output_map, 1 - parity, 1)[0],
            jnp.zeros((LANES - rank_size, width), BF16),
        ],
        axis=0,
    ).T
    outgoing, sent_weight = lax.optimization_barrier((outgoing, sent_weight))
    pair_weight = lax.ppermute(sent_weight, "tensor", swap)
    arrived = lax.all_to_all(
        outgoing, ("expert", "dp"), split_axis=0, concat_axis=0, tiled=True
    )
    adapter = lax.all_gather(adapter.astype(BF16), "expert")
    adapter = jnp.sum(adapter.astype(F32), axis=0).astype(BF16)
    arrived, adapter = lax.optimization_barrier((arrived, adapter))

    steps = 4
    fan = expert_hidden // steps
    part, own_rows, pair_rows, rank_part = pl.pallas_call(
        functools.partial(routed_kernel, hidden_local),
        grid_spec=pltpu.PrefetchScalarGridSpec(
            num_scalar_prefetch=1,
            grid=(steps,),
            in_specs=[
                pl.BlockSpec((group_count * 8, block_width), lambda j, p: (0, 0)),
                pl.BlockSpec((1, width, fan), lambda j, p: (p[0], 0, j)),
                pl.BlockSpec((width, fan), lambda j, p: (0, j)),
                pl.BlockSpec((1, rank_size, width), lambda j, p: (p[0], 0, 0)),
                pl.BlockSpec((width, LANES), lambda j, p: (0, expert_hidden // LANES)),
                pl.BlockSpec((rank_size, LANES), lambda j, p: (0, 0)),
            ],
            out_specs=(
                pl.BlockSpec((fan, slot_count), lambda j, p: (j, 0)),
                pl.BlockSpec((slot_count, width), lambda j, p: (0, 0)),
                pl.BlockSpec((slot_count, width), lambda j, p: (0, 0)),
                pl.BlockSpec((rank_size, slot_count + LANES), lambda j, p: (0, 0)),
            ),
        ),
        out_shape=(
            pltpu.HBM((expert_hidden, slot_count), BF16),
            pltpu.HBM((slot_count, width), BF16),
            pltpu.HBM((slot_count, width), BF16),
            jax.ShapeDtypeStruct((rank_size, slot_count + LANES), BF16),
        ),
        name="routed",
        compiler_params=pltpu.CompilerParams(vmem_limit_bytes=48 * 1024 * 1024),
    )(
        parity_scalar,
        arrived,
        jnp.swapaxes(routed_down_weight, 1, 2),
        pair_weight,
        routed_adapter_output_map,
        pair_weight,
        inner_chunk,
    )
    part, rank_part, token_rows, adapter = lax.optimization_barrier(
        (part, rank_part, token_rows, adapter)
    )
    reduced = lax.psum_scatter(
        part, "tensor", scatter_dimension=0, axis_index_groups=same_parity, tiled=True
    )
    taken = lax.ppermute(reduced[:hidden_local], "tensor", swap)
    kept = reduced[hidden_local:]
    hidden_gradient = jnp.stack(
        [jnp.where(even, kept, taken), jnp.where(even, taken, kept)], axis=1
    )

    gathered = lax.all_gather(rank_part, "tensor", axis=0, tiled=True).reshape(
        n_tensor, rank_size, -1
    )
    adapter = scale * jnp.sum(lax.all_gather(adapter, "dp").astype(F32), axis=0)
    grad_a_shared = adapter[:, :shared_local].T
    grad_b_shared = adapter[:, shared_local:]
    routed_rank = jnp.sum(
        gathered[:, :, :slot_count]
        .reshape(n_tensor // 2, expert_local, rank_size, slot_count)
        .astype(F32),
        axis=0,
    ).astype(BF16)
    chunks = slot_count // LANES
    inner_chunks = gathered[:, :, slot_count:]
    own_inner = pick(inner_chunks, parity, chunks)
    own_inner = jnp.swapaxes(own_inner, 0, 1).reshape(rank_size, slot_count)
    _, shared_gate_factor, shared_activated = swiglu_parts(
        shared_gate_saved[0], shared_up_saved[0]
    )
    shared_gradient = lax.dot_general(
        token_rows, shared_down_weight, contract_trailing, preferred_element_type=F32
    )
    shared_gradient = shared_gradient + ADAPTER_SCALE * lax.dot_general(
        shared_rank, shared_adapter_input_map, contract_trailing, preferred_element_type=F32
    )
    grad_gate_shared = (shared_gradient * shared_gate_factor).astype(BF16)[None]
    grad_up_shared = (shared_gradient * shared_activated).astype(BF16)[None]

    grad_a_routed = scale * jnp.einsum(
        "fes,ers->efr", routed_hidden, routed_rank, preferred_element_type=F32
    )
    own_b = scale * jnp.dot(own_inner, own_rows, preferred_element_type=F32)
    pair_b = scale * jnp.dot(own_inner, pair_rows, preferred_element_type=F32)
    pair_b = lax.ppermute(pair_b, "tensor", swap)
    grad_b_routed = jnp.stack([jnp.where(even, own_b, pair_b), jnp.where(even, pair_b, own_b)])
    low_rank = ADAPTER_SCALE * jnp.einsum(
        "ers,efr->fes", routed_rank, routed_adapter_input_map, preferred_element_type=F32
    )
    hidden_gradient = hidden_gradient.astype(F32) + low_rank
    grad_gate_routed = (hidden_gradient * routed_gate_factor).astype(BF16)
    grad_up_routed = (hidden_gradient * routed_activated).astype(BF16)
    return (
        grad_gate_routed,
        grad_up_routed,
        grad_gate_shared,
        grad_up_shared,
        grad_a_routed,
        grad_b_routed,
        grad_a_shared,
        grad_b_shared,
    )


def solution(mesh):
    placed = (
        P(("expert", "dp"), "tensor", None),
        P(("expert", "dp"), None, None),
        P(("expert", "dp"), None, None),
        P(("expert", "dp"), None, "tensor"),
        P(("expert", "dp"), "tensor", None),
        P(("expert", "dp"), None, "tensor"),
        P("tensor", ("expert", "dp"), None),
        P("tensor", ("expert", "dp"), None),
        P("tensor", None),
        P("tensor", None),
        P(),
        P(("expert", "dp"), None, "tensor"),
        P(("expert", "dp"), None, "tensor"),
    )
    return jax.shard_map(
        shards,
        mesh=mesh,
        in_specs=placed,
        out_specs=(
            P("tensor", ("expert", "dp"), None),
            P("tensor", ("expert", "dp"), None),
            P(("expert", "dp"), None, "tensor"),
            P(("expert", "dp"), None, "tensor"),
            P(("expert", "dp"), "tensor", None),
            P(("expert", "dp"), None, "tensor"),
            P("tensor", None),
            P(None, "tensor"),
        ),
        check_vma=False,
    )
```

```python
import functools

import jax
import jax.numpy as jnp
from jax import lax
from jax.experimental import pallas as pl
from jax.experimental.pallas import tpu as pltpu
from jax.sharding import PartitionSpec as P

ADAPTER_SCALE = 2.0
F32 = jnp.float32
BF16 = jnp.bfloat16
LANES = 128


def swiglu_parts(gate_value, up_value):
    gate_float = gate_value.astype(F32)
    up_float = up_value.astype(F32)
    sigmoid_gate = jax.nn.sigmoid(gate_float)
    activated = gate_float * sigmoid_gate
    hidden_state = (activated * up_float).astype(BF16)
    gate_factor = up_float * sigmoid_gate * (1.0 + gate_float * (1.0 - sigmoid_gate))
    return (hidden_state, gate_factor, activated)


def whole(count):
    return [pl.BlockSpec(memory_space=pltpu.VMEM)] * count


def pack_kernel(
    cot_ref,
    routed_ref,
    routed_map_ref,
    gate_ref,
    up_ref,
    shared_map_ref,
    map_ref,
    out_ref,
    hidden_ref,
    small_ref,
):
    n_tensor = out_ref.shape[0] // 8
    width = cot_ref.shape[1] // n_tensor
    per_expert = routed_ref.shape[2] // LANES
    experts = routed_ref.shape[0]
    inner = [
        jnp.dot(routed_map_ref[e], routed_ref[e], preferred_element_type=F32)
        for e in range(experts)
    ]
    hidden = swiglu_parts(gate_ref[...], up_ref[...])[0]
    hidden_ref[...] = hidden
    shared = lax.dot_general(
        shared_map_ref[...], hidden, (((1,), (1,)), ((), ())), preferred_element_type=F32
    )

    def chunk(t):
        if t // experts < per_expert:
            column = t // experts * LANES
            return inner[t % experts][:, column : column + LANES]
        return jnp.zeros((16, LANES), F32)

    rank = lax.dot_general(
        cot_ref[...], map_ref[...], (((1,), (1,)), ((), ())), preferred_element_type=F32
    )
    rank = jnp.concatenate([rank, jnp.zeros((8, LANES - rank.shape[1]), F32)], axis=1)
    small_ref[...] = jnp.concatenate([shared, rank, jnp.zeros((8, LANES), F32)], axis=0).astype(BF16)

    for pair in range(n_tensor // 2):
        rows = pl.ds(16 * pair, 16)
        both = cot_ref[:, 2 * pair * width : 2 * (pair + 1) * width].astype(F32)
        swapped = jnp.concatenate([both[:, width:], both[:, :width]], axis=1)
        out_ref[rows, 0 : 2 * width] = jnp.concatenate([both, swapped], axis=0).astype(BF16)
        first, second = chunk(2 * pair), chunk(2 * pair + 1)
        low = jnp.concatenate([first[0:8], second[0:8]], axis=0)
        high = jnp.concatenate([first[8:16], second[8:16]], axis=0)
        out_ref[rows, 2 * width : 2 * width + LANES] = low.astype(BF16)
        out_ref[rows, 2 * width + LANES : 2 * width + 2 * LANES] = high.astype(BF16)


def dispatch_kernel(
    parity_ref,
    index_ref,
    weight_ref,
    packed_ref,
    out_ref,
    chunk_ref,
    columns_ref,
):
    tokens = packed_ref.shape[0]
    width = columns_ref.shape[1]
    top = index_ref.shape[0]
    peers = out_ref.shape[0] // 8
    own = packed_ref[:, 0:width]
    other = packed_ref[:, width : 2 * width]

    columns_ref[...] = own
    halves = []
    for lane in (2 * width, 2 * width + LANES):
        partial = packed_ref[:, lane : lane + LANES].astype(F32)
        halves.append(jnp.sum(partial.reshape(tokens // 8, 8, LANES), axis=0))
    chunk_ref[...] = jnp.concatenate(halves, axis=0).astype(BF16)
    before = (
        lax.broadcasted_iota(jnp.int32, (tokens, tokens), 0)
        < lax.broadcasted_iota(jnp.int32, (tokens, tokens), 1)
    ).astype(BF16)
    expert = 2 * lax.broadcasted_iota(jnp.int32, (peers, tokens), 0) + parity_ref[0]
    weight = jnp.zeros((peers, tokens), F32)
    named = jnp.zeros((peers, tokens), F32)
    for k in range(top):
        match = expert == index_ref[k : k + 1, :]
        weight = jnp.where(match, weight_ref[k : k + 1, :], weight)
        named = jnp.where(match, 1.0, named)
    slot = jnp.dot(named.astype(BF16), before, preferred_element_type=F32)
    shape = (peers, 8, tokens)
    row = lax.broadcasted_iota(jnp.int32, shape, 1)
    slot = jnp.broadcast_to(slot[:, None, :], shape)
    weight = jnp.broadcast_to(weight[:, None, :], shape)

    def split(selector):
        selector = selector.reshape(peers * 8, tokens)
        high = selector.astype(BF16)
        return high, (selector - high.astype(F32)).astype(BF16)

    high, low = split(jnp.where(slot == row.astype(F32), weight, 0.0))
    left = jnp.concatenate([high, low], axis=1)
    both = packed_ref[:, 0 : 2 * width]
    right = jnp.concatenate([both, both], axis=0)
    out_ref[:, 0 : 2 * width] = jnp.dot(left, right, preferred_element_type=F32).astype(BF16)
    wanted = jnp.where(row < 4, row + 8, row + 4).astype(F32)
    tail = jnp.where(slot == wanted, weight, 0.0)
    first = split(jnp.where(row < 4, tail, 0.0))
    second = split(jnp.where(row < 4, 0.0, tail))
    left = jnp.concatenate([first[0], first[1], second[0], second[1]], axis=1)
    right = jnp.concatenate([own, own, other, other], axis=0)
    out_ref[:, 2 * width : 3 * width] = jnp.dot(left, right, preferred_element_type=F32).astype(BF16)
    rest = out_ref.shape[1] - 3 * width
    out_ref[:, 3 * width :] = jnp.zeros((peers * 8, rest), BF16)


def adapter_kernel(small_ref, columns_ref, hidden_ref, adapter_ref, rank_ref):
    parts = small_ref[...].astype(F32).reshape(-1, 32, LANES)
    shared_inner = jnp.sum(parts[:, 0:16, :], axis=0).astype(BF16)
    shared_rank = parts[:, 16:24, :].reshape(rank_ref.shape).astype(BF16)
    rank_ref[...] = shared_rank
    adapter_a = lax.dot_general(
        shared_rank, hidden_ref[...], (((0,), (0,)), ((), ())), preferred_element_type=F32
    )
    adapter_b = jnp.dot(shared_inner, columns_ref[...], preferred_element_type=F32)
    local = hidden_ref.shape[1]
    adapter_ref[:, 0:local] = adapter_a[0 : adapter_ref.shape[0]].astype(BF16)
    adapter_ref[:, local:] = adapter_b.astype(BF16)


def routed_kernel(
    hidden_local,
    parity_ref,
    arrived_ref,
    own_weight_ref,
    pair_weight_ref,
    own_map_ref,
    pair_map_ref,
    chunk_ref,
    part_ref,
    own_rows_ref,
    pair_rows_ref,
    gather_ref,
):
    slots, width = own_rows_ref.shape
    block, groups = 192, 16
    turned = (((0,), (1,)), ((), ()))

    @pl.when(pl.program_id(0) == 0)
    def _():
        i = lax.broadcasted_iota(jnp.int32, (block, 8 * groups), 0)
        j = lax.broadcasted_iota(jnp.int32, (block, 8 * groups), 1)
        group = lax.shift_right_logical(i * 5462, 16)
        slot = i - 12 * group
        head = (j == 8 * group + slot) & (slot < 8)
        for half, rows_ref in enumerate((own_rows_ref, pair_rows_ref)):
            tail = (j == 8 * group + slot - 8 + 4 * half) & (slot >= 8)
            pick = jnp.concatenate([head.astype(F32), tail.astype(F32)], axis=1).astype(BF16)
            for b in range(slots // block):
                rows = pl.ds(8 * groups * b, 8 * groups)
                source = jnp.concatenate(
                    [
                        arrived_ref[rows, half * width : (half + 1) * width],
                        arrived_ref[rows, 2 * width : 3 * width],
                    ],
                    axis=0,
                )
                rows_ref[block * b : block * (b + 1), :] = jnp.dot(
                    pick, source, preferred_element_type=F32
                ).astype(BF16)
        rank = lax.dot_general(
            own_map_ref[0], own_rows_ref[...], (((1,), (1,)), ((), ())), preferred_element_type=F32
        )
        pair_rank = lax.dot_general(
            pair_map_ref[...], pair_rows_ref[...], turned, preferred_element_type=F32
        )
        gather_ref[:, 0:slots] = (rank + pair_rank[0 : rank.shape[0]]).astype(BF16)
        gather_ref[:, slots : slots + LANES] = chunk_ref[...]

    part = lax.dot_general(
        own_weight_ref[0], own_rows_ref[...], turned, preferred_element_type=F32
    ) + lax.dot_general(
        pair_weight_ref[...], pair_rows_ref[...], turned, preferred_element_type=F32
    )
    flip = 1 - parity_ref[0]
    for b in range(part.shape[0] // hidden_local):
        start = pl.multiple_of((b ^ flip) * hidden_local, hidden_local)
        part_ref[pl.ds(start, hidden_local), :] = part[
            b * hidden_local : (b + 1) * hidden_local
        ].astype(BF16)


def shards(
    cotangent,
    routed_expert_index,
    chosen_gate_weight,
    routed_down_weight,
    routed_adapter_input_map,
    routed_adapter_output_map,
    routed_gate_saved,
    routed_up_saved,
    shared_down_weight,
    shared_adapter_input_map,
    shared_adapter_output_map,
    shared_gate_saved,
    shared_up_saved,
):
    n_tensor = lax.axis_size("tensor")
    group_count = lax.axis_size("expert") * lax.axis_size("dp")
    expert_local, expert_hidden, width = routed_down_weight.shape
    hidden_local = expert_hidden // n_tensor
    slot_count = routed_gate_saved.shape[2]
    rank_size = routed_adapter_output_map.shape[1]
    scale = ADAPTER_SCALE / group_count
    contract_trailing = (((1,), (1,)), ((), ()))
    parity = lax.bitwise_and(lax.axis_index("tensor"), 1)
    even = parity == 0
    parity_scalar = parity.reshape(1)
    swap = [(t, t ^ 1) for t in range(n_tensor)]
    same_parity = [list(range(p, n_tensor, 2)) for p in range(2)]

    def pick(array, index, size):
        return lax.dynamic_slice_in_dim(array, index * size, size, 0, allow_negative_indices=False)

    token_rows = lax.all_gather(cotangent, "tensor", axis=1, tiled=True)[0]
    tokens = token_rows.shape[0]

    routed_hidden, routed_gate_factor, routed_activated = swiglu_parts(
        routed_gate_saved, routed_up_saved
    )
    shared_local = shared_gate_saved.shape[2]
    packed, shared_hidden, small = pl.pallas_call(
        pack_kernel,
        out_shape=(
            jax.ShapeDtypeStruct((8 * n_tensor, 2 * width + 2 * LANES), BF16),
            jax.ShapeDtypeStruct((tokens, shared_local), BF16),
            jax.ShapeDtypeStruct((32, LANES), BF16),
        ),
        in_specs=whole(7),
        out_specs=tuple(whole(3)),
        name="pack",
    )(
        cotangent[0],
        jnp.swapaxes(routed_hidden, 0, 1),
        jnp.swapaxes(routed_adapter_input_map, 1, 2),
        shared_gate_saved[0],
        shared_up_saved[0],
        shared_adapter_input_map.T,
        shared_adapter_output_map,
    )
    packed = lax.all_to_all(packed, "tensor", split_axis=0, concat_axis=0, tiled=True)

    block_width = -(-3 * width // LANES) * LANES
    outgoing, inner_chunk, own_columns = pl.pallas_call(
        dispatch_kernel,
        out_shape=(
            pltpu.HBM((group_count * 8, block_width), BF16),
            jax.ShapeDtypeStruct((rank_size, LANES), BF16),
            jax.ShapeDtypeStruct((tokens, width), BF16),
        ),
        in_specs=[pl.BlockSpec(memory_space=pltpu.SMEM)] + whole(3),
        out_specs=(pl.BlockSpec((group_count * 8, block_width), lambda: (0, 0)), *whole(2)),
        name="dispatch",
        compiler_params=pltpu.CompilerParams(vmem_limit_bytes=32 * 1024 * 1024),
    )(parity_scalar, routed_expert_index[0].T, chosen_gate_weight[0].T, packed)

    sent_weight = jnp.concatenate(
        [
            pick(routed_down_weight, 1 - parity, 1)[0],
            pick(routed_adapter_output_map, 1 - parity, 1)[0],
            jnp.zeros((LANES - rank_size, width), BF16),
        ],
        axis=0,
    ).T
    outgoing, sent_weight = lax.optimization_barrier((outgoing, sent_weight))
    pair_weight = lax.ppermute(sent_weight, "tensor", swap)
    arrived = lax.all_to_all(
        outgoing, ("expert", "dp"), split_axis=0, concat_axis=0, tiled=True
    )
    adapter, shared_rank = pl.pallas_call(
        adapter_kernel,
        out_shape=(
            jax.ShapeDtypeStruct((rank_size, shared_local + width), BF16),
            jax.ShapeDtypeStruct((tokens, LANES), BF16),
        ),
        in_specs=whole(3),
        out_specs=tuple(whole(2)),
        name="adapter",
    )(lax.all_gather(small, "tensor", axis=0, tiled=True), own_columns, shared_hidden)
    arrived, adapter, shared_rank = lax.optimization_barrier((arrived, adapter, shared_rank))
    shared_rank = shared_rank[:, :rank_size]

    steps = 4
    fan = expert_hidden // steps
    part, own_rows, pair_rows, rank_part = pl.pallas_call(
        functools.partial(routed_kernel, hidden_local),
        grid_spec=pltpu.PrefetchScalarGridSpec(
            num_scalar_prefetch=1,
            grid=(steps,),
            in_specs=[
                pl.BlockSpec((group_count * 8, block_width), lambda j, p: (0, 0)),
                pl.BlockSpec((1, width, fan), lambda j, p: (p[0], 0, j)),
                pl.BlockSpec((width, fan), lambda j, p: (0, j)),
                pl.BlockSpec((1, rank_size, width), lambda j, p: (p[0], 0, 0)),
                pl.BlockSpec((width, LANES), lambda j, p: (0, expert_hidden // LANES)),
                pl.BlockSpec((rank_size, LANES), lambda j, p: (0, 0)),
            ],
            out_specs=(
                pl.BlockSpec((fan, slot_count), lambda j, p: (j, 0)),
                pl.BlockSpec((slot_count, width), lambda j, p: (0, 0)),
                pl.BlockSpec((slot_count, width), lambda j, p: (0, 0)),
                pl.BlockSpec((rank_size, slot_count + LANES), lambda j, p: (0, 0)),
            ),
        ),
        out_shape=(
            pltpu.HBM((expert_hidden, slot_count), BF16),
            pltpu.HBM((slot_count, width), BF16),
            pltpu.HBM((slot_count, width), BF16),
            jax.ShapeDtypeStruct((rank_size, slot_count + LANES), BF16),
        ),
        name="routed",
        compiler_params=pltpu.CompilerParams(vmem_limit_bytes=48 * 1024 * 1024),
    )(
        parity_scalar,
        arrived,
        jnp.swapaxes(routed_down_weight, 1, 2),
        pair_weight,
        routed_adapter_output_map,
        pair_weight,
        inner_chunk,
    )
    part, rank_part, token_rows, adapter = lax.optimization_barrier(
        (part, rank_part, token_rows, adapter)
    )
    reduced = lax.psum_scatter(
        part, "tensor", scatter_dimension=0, axis_index_groups=same_parity, tiled=True
    )
    taken = lax.ppermute(reduced[:hidden_local], "tensor", swap)
    kept = reduced[hidden_local:]
    hidden_gradient = jnp.stack(
        [jnp.where(even, kept, taken), jnp.where(even, taken, kept)], axis=1
    )

    gathered = lax.all_gather(
        rank_part, "tensor", axis=0, axis_index_groups=same_parity, tiled=True
    ).reshape(n_tensor // 2, rank_size, -1)
    own_rank = jnp.sum(gathered[:, :, :slot_count].astype(F32), axis=0).astype(BF16)
    own_inner = jnp.swapaxes(gathered[: slot_count // LANES, :, slot_count:], 0, 1)
    own_inner = own_inner.reshape(rank_size, slot_count)
    own_b = scale * jnp.dot(own_inner, own_rows, preferred_element_type=F32)
    pair_b = scale * jnp.dot(own_inner, pair_rows, preferred_element_type=F32)
    swapped = jnp.concatenate([own_rank, pair_b.astype(BF16)], axis=1)
    swapped = lax.ppermute(swapped, "tensor", swap)
    pair_rank, pair_b = swapped[:, :slot_count], swapped[:, slot_count:].astype(F32)
    routed_rank = jnp.stack(
        [jnp.where(even, own_rank, pair_rank), jnp.where(even, pair_rank, own_rank)]
    )
    grad_b_routed = jnp.stack([jnp.where(even, own_b, pair_b), jnp.where(even, pair_b, own_b)])

    adapter = jnp.sum(lax.all_gather(adapter, "expert").astype(F32), axis=0).astype(BF16)
    adapter = scale * jnp.sum(lax.all_gather(adapter, "dp").astype(F32), axis=0)
    grad_a_shared = adapter[:, :shared_local].T
    grad_b_shared = adapter[:, shared_local:]

    _, shared_gate_factor, shared_activated = swiglu_parts(
        shared_gate_saved[0], shared_up_saved[0]
    )
    shared_gradient = lax.dot_general(
        token_rows, shared_down_weight, contract_trailing, preferred_element_type=F32
    )
    shared_gradient = shared_gradient + ADAPTER_SCALE * lax.dot_general(
        shared_rank, shared_adapter_input_map, contract_trailing, preferred_element_type=F32
    )
    grad_gate_shared = (shared_gradient * shared_gate_factor).astype(BF16)[None]
    grad_up_shared = (shared_gradient * shared_activated).astype(BF16)[None]

    grad_a_routed = scale * jnp.einsum(
        "fes,ers->efr", routed_hidden, routed_rank, preferred_element_type=F32
    )
    low_rank = ADAPTER_SCALE * jnp.einsum(
        "ers,efr->fes", routed_rank, routed_adapter_input_map, preferred_element_type=F32
    )
    hidden_gradient = hidden_gradient.astype(F32) + low_rank
    grad_gate_routed = (hidden_gradient * routed_gate_factor).astype(BF16)
    grad_up_routed = (hidden_gradient * routed_activated).astype(BF16)
    return (
        grad_gate_routed,
        grad_up_routed,
        grad_gate_shared,
        grad_up_shared,
        grad_a_routed,
        grad_b_routed,
        grad_a_shared,
        grad_b_shared,
    )


def solution(mesh):
    placed = (
        P(("expert", "dp"), "tensor", None),
        P(("expert", "dp"), None, None),
        P(("expert", "dp"), None, None),
        P(("expert", "dp"), None, "tensor"),
        P(("expert", "dp"), "tensor", None),
        P(("expert", "dp"), None, "tensor"),
        P("tensor", ("expert", "dp"), None),
        P("tensor", ("expert", "dp"), None),
        P("tensor", None),
        P("tensor", None),
        P(),
        P(("expert", "dp"), None, "tensor"),
        P(("expert", "dp"), None, "tensor"),
    )
    return jax.shard_map(
        shards,
        mesh=mesh,
        in_specs=placed,
        out_specs=(
            P("tensor", ("expert", "dp"), None),
            P("tensor", ("expert", "dp"), None),
            P(("expert", "dp"), None, "tensor"),
            P(("expert", "dp"), None, "tensor"),
            P(("expert", "dp"), "tensor", None),
            P(("expert", "dp"), None, "tensor"),
            P("tensor", None),
            P(None, "tensor"),
        ),
        check_vma=False,
    )
```

```python
import functools

import jax
import jax.numpy as jnp
from jax import lax
from jax.experimental import pallas as pl
from jax.experimental.pallas import tpu as pltpu
from jax.sharding import PartitionSpec as P

ADAPTER_SCALE = 2.0
F32 = jnp.float32
BF16 = jnp.bfloat16
LANES = 128


def swiglu_parts(gate_value, up_value):
    gate_float = gate_value.astype(F32)
    up_float = up_value.astype(F32)
    sigmoid_gate = jax.nn.sigmoid(gate_float)
    activated = gate_float * sigmoid_gate
    hidden_state = (activated * up_float).astype(BF16)
    gate_factor = up_float * sigmoid_gate * (1.0 + gate_float * (1.0 - sigmoid_gate))
    return (hidden_state, gate_factor, activated)


def whole(count):
    return [pl.BlockSpec(memory_space=pltpu.VMEM)] * count


def pack_kernel(
    cot_ref,
    routed_ref,
    routed_map_ref,
    gate_ref,
    up_ref,
    shared_map_ref,
    map_ref,
    out_ref,
    hidden_ref,
):
    n_tensor = out_ref.shape[0] // 8
    width = cot_ref.shape[1] // n_tensor
    per_expert = routed_ref.shape[2] // LANES
    experts = routed_ref.shape[0]
    inner = [
        jnp.dot(routed_map_ref[e], routed_ref[e], preferred_element_type=F32)
        for e in range(experts)
    ]
    hidden = swiglu_parts(gate_ref[...], up_ref[...])[0]
    hidden_ref[...] = hidden
    shared = lax.dot_general(
        shared_map_ref[...], hidden, (((1,), (1,)), ((), ())), preferred_element_type=F32
    )

    def chunk(t):
        if t // experts < per_expert:
            column = t // experts * LANES
            return inner[t % experts][:, column : column + LANES]
        return jnp.zeros((16, LANES), F32)

    rank = lax.dot_general(
        cot_ref[...], map_ref[...], (((1,), (1,)), ((), ())), preferred_element_type=F32
    )
    rank = jnp.concatenate([rank, jnp.zeros((8, LANES - rank.shape[1]), F32)], axis=1)
    common = [shared[0:8], shared[8:16], rank]
    common = [jnp.concatenate([x, x], axis=0).astype(BF16) for x in common]

    for pair in range(n_tensor // 2):
        rows = pl.ds(16 * pair, 16)
        both = cot_ref[:, 2 * pair * width : 2 * (pair + 1) * width].astype(F32)
        swapped = jnp.concatenate([both[:, width:], both[:, :width]], axis=1)
        out_ref[rows, 0 : 2 * width] = jnp.concatenate([both, swapped], axis=0).astype(BF16)
        first, second = chunk(2 * pair), chunk(2 * pair + 1)
        low = jnp.concatenate([first[0:8], second[0:8]], axis=0)
        high = jnp.concatenate([first[8:16], second[8:16]], axis=0)
        out_ref[rows, 2 * width : 2 * width + LANES] = low.astype(BF16)
        out_ref[rows, 2 * width + LANES : 2 * width + 2 * LANES] = high.astype(BF16)
        for n, x in enumerate(common):
            lane = 2 * width + (2 + n) * LANES
            out_ref[rows, lane : lane + LANES] = x


def dispatch_kernel(
    parity_ref,
    index_ref,
    weight_ref,
    packed_ref,
    hidden_ref,
    out_ref,
    chunk_ref,
    rank_ref,
    adapter_ref,
):
    tokens = packed_ref.shape[0]
    width = adapter_ref.shape[1] - hidden_ref.shape[1]
    top = index_ref.shape[0]
    peers = out_ref.shape[0] // 8
    own = packed_ref[:, 0:width]
    other = packed_ref[:, width : 2 * width]

    def summed(lane):
        halves = []
        for first in (lane, lane + LANES):
            partial = packed_ref[:, first : first + LANES].astype(F32)
            halves.append(jnp.sum(partial.reshape(tokens // 8, 8, LANES), axis=0))
        return jnp.concatenate(halves, axis=0).astype(BF16)

    chunk_ref[...] = summed(2 * width)
    shared_inner = summed(2 * width + 2 * LANES)
    shared_rank = packed_ref[:, 2 * width + 4 * LANES : 2 * width + 5 * LANES]
    rank_ref[...] = shared_rank
    adapter_a = lax.dot_general(
        shared_rank, hidden_ref[...], (((0,), (0,)), ((), ())), preferred_element_type=F32
    )
    adapter_ref[:, 0 : hidden_ref.shape[1]] = adapter_a[0 : adapter_ref.shape[0]]
    adapter_ref[:, hidden_ref.shape[1] :] = jnp.dot(
        shared_inner, own, preferred_element_type=F32
    )
    before = (
        lax.broadcasted_iota(jnp.int32, (tokens, tokens), 0)
        < lax.broadcasted_iota(jnp.int32, (tokens, tokens), 1)
    ).astype(BF16)
    expert = 2 * lax.broadcasted_iota(jnp.int32, (peers, tokens), 0) + parity_ref[0]
    weight = jnp.zeros((peers, tokens), F32)
    named = jnp.zeros((peers, tokens), F32)
    for k in range(top):
        match = expert == index_ref[k : k + 1, :]
        weight = jnp.where(match, weight_ref[k : k + 1, :], weight)
        named = jnp.where(match, 1.0, named)
    slot = jnp.dot(named.astype(BF16), before, preferred_element_type=F32)
    shape = (peers, 8, tokens)
    row = lax.broadcasted_iota(jnp.int32, shape, 1)
    slot = jnp.broadcast_to(slot[:, None, :], shape)
    weight = jnp.broadcast_to(weight[:, None, :], shape)

    def split(selector):
        selector = selector.reshape(peers * 8, tokens)
        high = selector.astype(BF16)
        return high, (selector - high.astype(F32)).astype(BF16)

    high, low = split(jnp.where(slot == row.astype(F32), weight, 0.0))
    left = jnp.concatenate([high, low], axis=1)
    both = packed_ref[:, 0 : 2 * width]
    right = jnp.concatenate([both, both], axis=0)
    out_ref[:, 0 : 2 * width] = jnp.dot(left, right, preferred_element_type=F32).astype(BF16)
    wanted = jnp.where(row < 4, row + 8, row + 4).astype(F32)
    tail = jnp.where(slot == wanted, weight, 0.0)
    first = split(jnp.where(row < 4, tail, 0.0))
    second = split(jnp.where(row < 4, 0.0, tail))
    left = jnp.concatenate([first[0], first[1], second[0], second[1]], axis=1)
    right = jnp.concatenate([own, own, other, other], axis=0)
    out_ref[:, 2 * width : 3 * width] = jnp.dot(left, right, preferred_element_type=F32).astype(BF16)
    rest = out_ref.shape[1] - 3 * width
    out_ref[:, 3 * width :] = jnp.zeros((peers * 8, rest), BF16)


def routed_kernel(
    hidden_local,
    parity_ref,
    arrived_ref,
    own_weight_ref,
    pair_weight_ref,
    own_map_ref,
    pair_map_ref,
    chunk_ref,
    part_ref,
    own_rows_ref,
    pair_rows_ref,
    gather_ref,
):
    slots, width = own_rows_ref.shape
    block, groups = 192, 16
    turned = (((0,), (1,)), ((), ()))

    @pl.when(pl.program_id(0) == 0)
    def _():
        i = lax.broadcasted_iota(jnp.int32, (block, 8 * groups), 0)
        j = lax.broadcasted_iota(jnp.int32, (block, 8 * groups), 1)
        group = lax.shift_right_logical(i * 5462, 16)
        slot = i - 12 * group
        head = (j == 8 * group + slot) & (slot < 8)
        for half, rows_ref in enumerate((own_rows_ref, pair_rows_ref)):
            tail = (j == 8 * group + slot - 8 + 4 * half) & (slot >= 8)
            pick = jnp.concatenate([head.astype(F32), tail.astype(F32)], axis=1).astype(BF16)
            for b in range(slots // block):
                rows = pl.ds(8 * groups * b, 8 * groups)
                source = jnp.concatenate(
                    [
                        arrived_ref[rows, half * width : (half + 1) * width],
                        arrived_ref[rows, 2 * width : 3 * width],
                    ],
                    axis=0,
                )
                rows_ref[block * b : block * (b + 1), :] = jnp.dot(
                    pick, source, preferred_element_type=F32
                ).astype(BF16)
        rank = lax.dot_general(
            own_map_ref[0], own_rows_ref[...], (((1,), (1,)), ((), ())), preferred_element_type=F32
        )
        pair_rank = lax.dot_general(
            pair_map_ref[...], pair_rows_ref[...], turned, preferred_element_type=F32
        )
        gather_ref[:, 0:slots] = (rank + pair_rank[0 : rank.shape[0]]).astype(BF16)
        gather_ref[:, slots : slots + LANES] = chunk_ref[...]

    part = lax.dot_general(
        own_weight_ref[0], own_rows_ref[...], turned, preferred_element_type=F32
    ) + lax.dot_general(
        pair_weight_ref[...], pair_rows_ref[...], turned, preferred_element_type=F32
    )
    flip = 1 - parity_ref[0]
    for b in range(part.shape[0] // hidden_local):
        start = pl.multiple_of((b ^ flip) * hidden_local, hidden_local)
        part_ref[pl.ds(start, hidden_local), :] = part[
            b * hidden_local : (b + 1) * hidden_local
        ].astype(BF16)


def shards(
    cotangent,
    routed_expert_index,
    chosen_gate_weight,
    routed_down_weight,
    routed_adapter_input_map,
    routed_adapter_output_map,
    routed_gate_saved,
    routed_up_saved,
    shared_down_weight,
    shared_adapter_input_map,
    shared_adapter_output_map,
    shared_gate_saved,
    shared_up_saved,
):
    n_tensor = lax.axis_size("tensor")
    group_count = lax.axis_size("expert") * lax.axis_size("dp")
    expert_local, expert_hidden, width = routed_down_weight.shape
    hidden_local = expert_hidden // n_tensor
    slot_count = routed_gate_saved.shape[2]
    rank_size = routed_adapter_output_map.shape[1]
    scale = ADAPTER_SCALE / group_count
    contract_trailing = (((1,), (1,)), ((), ()))
    parity = lax.bitwise_and(lax.axis_index("tensor"), 1)
    even = parity == 0
    parity_scalar = parity.reshape(1)
    swap = [(t, t ^ 1) for t in range(n_tensor)]
    same_parity = [list(range(p, n_tensor, 2)) for p in range(2)]

    def pick(array, index, size):
        return lax.dynamic_slice_in_dim(array, index * size, size, 0, allow_negative_indices=False)

    token_rows = lax.all_gather(cotangent, "tensor", axis=1, tiled=True)[0]
    tokens = token_rows.shape[0]

    routed_hidden, routed_gate_factor, routed_activated = swiglu_parts(
        routed_gate_saved, routed_up_saved
    )
    shared_local = shared_gate_saved.shape[2]
    packed, shared_hidden = pl.pallas_call(
        pack_kernel,
        out_shape=(
            jax.ShapeDtypeStruct((8 * n_tensor, 2 * width + 5 * LANES), BF16),
            jax.ShapeDtypeStruct((tokens, shared_local), BF16),
        ),
        in_specs=whole(7),
        out_specs=tuple(whole(2)),
        name="pack",
    )(
        cotangent[0],
        jnp.swapaxes(routed_hidden, 0, 1),
        jnp.swapaxes(routed_adapter_input_map, 1, 2),
        shared_gate_saved[0],
        shared_up_saved[0],
        shared_adapter_input_map.T,
        shared_adapter_output_map,
    )
    packed = lax.all_to_all(packed, "tensor", split_axis=0, concat_axis=0, tiled=True)

    block_width = -(-3 * width // LANES) * LANES
    outgoing, inner_chunk, shared_rank, adapter = pl.pallas_call(
        dispatch_kernel,
        out_shape=(
            jax.ShapeDtypeStruct((group_count * 8, block_width), BF16),
            jax.ShapeDtypeStruct((rank_size, LANES), BF16),
            jax.ShapeDtypeStruct((tokens, LANES), BF16),
            jax.ShapeDtypeStruct((rank_size, shared_local + width), F32),
        ),
        in_specs=[pl.BlockSpec(memory_space=pltpu.SMEM)] + whole(4),
        out_specs=tuple(whole(4)),
        name="dispatch",
        compiler_params=pltpu.CompilerParams(vmem_limit_bytes=32 * 1024 * 1024),
    )(parity_scalar, routed_expert_index[0].T, chosen_gate_weight[0].T, packed, shared_hidden)
    shared_rank = shared_rank[:, :rank_size]

    sent_weight = jnp.concatenate(
        [
            pick(routed_down_weight, 1 - parity, 1)[0],
            pick(routed_adapter_output_map, 1 - parity, 1)[0],
            jnp.zeros((LANES - rank_size, width), BF16),
        ],
        axis=0,
    ).T
    outgoing, sent_weight = lax.optimization_barrier((outgoing, sent_weight))
    pair_weight = lax.ppermute(sent_weight, "tensor", swap)
    arrived = lax.all_to_all(
        outgoing, ("expert", "dp"), split_axis=0, concat_axis=0, tiled=True
    )
    adapter = lax.all_gather(adapter.astype(BF16), "dp")
    adapter = jnp.sum(adapter.astype(F32), axis=0).astype(BF16)
    arrived, adapter = lax.optimization_barrier((arrived, adapter))

    steps = 4
    fan = expert_hidden // steps
    part, own_rows, pair_rows, rank_part = pl.pallas_call(
        functools.partial(routed_kernel, hidden_local),
        grid_spec=pltpu.PrefetchScalarGridSpec(
            num_scalar_prefetch=1,
            grid=(steps,),
            in_specs=[
                pl.BlockSpec((group_count * 8, block_width), lambda j, p: (0, 0)),
                pl.BlockSpec((1, width, fan), lambda j, p: (p[0], 0, j)),
                pl.BlockSpec((width, fan), lambda j, p: (0, j)),
                pl.BlockSpec((1, rank_size, width), lambda j, p: (p[0], 0, 0)),
                pl.BlockSpec((width, LANES), lambda j, p: (0, expert_hidden // LANES)),
                pl.BlockSpec((rank_size, LANES), lambda j, p: (0, 0)),
            ],
            out_specs=(
                pl.BlockSpec((fan, slot_count), lambda j, p: (j, 0)),
                pl.BlockSpec((slot_count, width), lambda j, p: (0, 0)),
                pl.BlockSpec((slot_count, width), lambda j, p: (0, 0)),
                pl.BlockSpec((rank_size, slot_count + LANES), lambda j, p: (0, 0)),
            ),
        ),
        out_shape=(
            pltpu.HBM((expert_hidden, slot_count), BF16),
            pltpu.HBM((slot_count, width), BF16),
            pltpu.HBM((slot_count, width), BF16),
            jax.ShapeDtypeStruct((rank_size, slot_count + LANES), BF16),
        ),
        name="routed",
        compiler_params=pltpu.CompilerParams(vmem_limit_bytes=48 * 1024 * 1024),
    )(
        parity_scalar,
        arrived,
        jnp.swapaxes(routed_down_weight, 1, 2),
        pair_weight,
        routed_adapter_output_map,
        pair_weight,
        inner_chunk,
    )
    part, rank_part, token_rows, adapter = lax.optimization_barrier(
        (part, rank_part, token_rows, adapter)
    )
    reduced = lax.psum_scatter(
        part, "tensor", scatter_dimension=0, axis_index_groups=same_parity, tiled=True
    )
    taken = lax.ppermute(reduced[:hidden_local], "tensor", swap)
    kept = reduced[hidden_local:]
    hidden_gradient = jnp.stack(
        [jnp.where(even, kept, taken), jnp.where(even, taken, kept)], axis=1
    )

    gathered = lax.all_gather(
        rank_part, "tensor", axis=0, axis_index_groups=same_parity, tiled=True
    ).reshape(n_tensor // 2, rank_size, -1)
    own_rank = jnp.sum(gathered[:, :, :slot_count].astype(F32), axis=0).astype(BF16)
    own_inner = jnp.swapaxes(gathered[: slot_count // LANES, :, slot_count:], 0, 1)
    own_inner = own_inner.reshape(rank_size, slot_count)
    own_b = scale * jnp.dot(own_inner, own_rows, preferred_element_type=F32)
    pair_b = scale * jnp.dot(own_inner, pair_rows, preferred_element_type=F32)
    swapped = jnp.concatenate([own_rank, pair_b.astype(BF16)], axis=1)
    swapped = lax.ppermute(swapped, "tensor", swap)
    pair_rank, pair_b = swapped[:, :slot_count], swapped[:, slot_count:].astype(F32)
    routed_rank = jnp.stack(
        [jnp.where(even, own_rank, pair_rank), jnp.where(even, pair_rank, own_rank)]
    )
    grad_b_routed = jnp.stack([jnp.where(even, own_b, pair_b), jnp.where(even, pair_b, own_b)])

    adapter = scale * jnp.sum(lax.all_gather(adapter, "expert").astype(F32), axis=0)
    grad_a_shared = adapter[:, :shared_local].T
    grad_b_shared = adapter[:, shared_local:]

    _, shared_gate_factor, shared_activated = swiglu_parts(
        shared_gate_saved[0], shared_up_saved[0]
    )
    shared_gradient = lax.dot_general(
        token_rows, shared_down_weight, contract_trailing, preferred_element_type=F32
    )
    shared_gradient = shared_gradient + ADAPTER_SCALE * lax.dot_general(
        shared_rank, shared_adapter_input_map, contract_trailing, preferred_element_type=F32
    )
    grad_gate_shared = (shared_gradient * shared_gate_factor).astype(BF16)[None]
    grad_up_shared = (shared_gradient * shared_activated).astype(BF16)[None]

    grad_a_routed = scale * jnp.einsum(
        "fes,ers->efr", routed_hidden, routed_rank, preferred_element_type=F32
    )
    low_rank = ADAPTER_SCALE * jnp.einsum(
        "ers,efr->fes", routed_rank, routed_adapter_input_map, preferred_element_type=F32
    )
    hidden_gradient = hidden_gradient.astype(F32) + low_rank
    grad_gate_routed = (hidden_gradient * routed_gate_factor).astype(BF16)
    grad_up_routed = (hidden_gradient * routed_activated).astype(BF16)
    return (
        grad_gate_routed,
        grad_up_routed,
        grad_gate_shared,
        grad_up_shared,
        grad_a_routed,
        grad_b_routed,
        grad_a_shared,
        grad_b_shared,
    )


def solution(mesh):
    placed = (
        P(("expert", "dp"), "tensor", None),
        P(("expert", "dp"), None, None),
        P(("expert", "dp"), None, None),
        P(("expert", "dp"), None, "tensor"),
        P(("expert", "dp"), "tensor", None),
        P(("expert", "dp"), None, "tensor"),
        P("tensor", ("expert", "dp"), None),
        P("tensor", ("expert", "dp"), None),
        P("tensor", None),
        P("tensor", None),
        P(),
        P(("expert", "dp"), None, "tensor"),
        P(("expert", "dp"), None, "tensor"),
    )
    return jax.shard_map(
        shards,
        mesh=mesh,
        in_specs=placed,
        out_specs=(
            P("tensor", ("expert", "dp"), None),
            P("tensor", ("expert", "dp"), None),
            P(("expert", "dp"), None, "tensor"),
            P(("expert", "dp"), None, "tensor"),
            P(("expert", "dp"), "tensor", None),
            P(("expert", "dp"), None, "tensor"),
            P("tensor", None),
            P(None, "tensor"),
        ),
        check_vma=False,
    )
```
